32 devices in a mesh: dp: 8 (over z, y), pipe: 4 (over x, core).
Axes of the slice: x: 2, y: 2, z: 4, core: 2. Of those that a mesh axis runs over, the one named last changes fastest.
Arguments:
- features: bfloat16 [2, 48, 13, 13, 512], P(None, 'dp', None, None, 'pipe'), may hold values from -6 to 6
- clip_counts: int32 [2, 16], P(None, 'dp'), may hold values from 1 to 3, as said below
- conv4_weight: bfloat16 [3, 3, 512, 512], replicated, may hold values from -0.09375 to 0.09375
- conv4_bias: float32 [512], replicated, may hold values from -3 to 3
- conv5_weight: bfloat16 [3, 3, 512, 512], replicated, may hold values from -0.09375 to 0.09375
- conv5_bias: float32 [512], replicated, may hold values from -3 to 3
- cotangent: bfloat16 [2, 48, 13, 13, 512], P(None, 'dp', None, None, 'pipe'), may hold values from -6 to 6
Outputs:
- conv5_out: bfloat16 [2, 48, 13, 13, 512], P(None, 'dp', None, None, 'pipe')
- input_grad: bfloat16 [2, 48, 13, 13, 512], P(None, 'dp', None, None, 'pipe')
- conv4_weight_grad: float32 [3, 3, 512, 512], P(None, None, 'pipe', 'dp')
- conv4_bias_grad: float32 [512], P('dp')
- conv5_weight_grad: float32 [3, 3, 512, 512], P(None, None, 'pipe', 'dp')
- conv5_bias_grad: float32 [512], P('dp')
The draws below stay inside these ranges and needn't reach their ends.
Inputs may be any that keep to these rules, and one draw needn't show every extreme that they name: `clip_counts`: each video's clips fill the next slots of its device's 6 slots in order, 2 videos a device and micro-batch.
All inputs are finite; a program needn't handle non-finite values.
Results may differ from the reference program's by a relative error of at most 0.012.
Values may be sent and summed in bfloat16 or wider, within the bound.
No kernel may reach another device: no remote copies, remote signals or barrier semaphores. Data moves between devices by JAX's collectives and lax.ppermute only.
A program may use at most 128 MiB of HBM per device.

```python
import jax
import jax.numpy as jnp
from jax import lax

CHANNELS = 512
SIDE = 13
MICRO = 2
MOST = 3
VIDS = 2
CAP = 6
ROWS = 48
N_DP = 8


def draw_clip_counts(key, part):
    key = jax.random.fold_in(key, 7)
    count_key, place_key = jax.random.split(key)
    counts = jax.random.randint(count_key, (MICRO, N_DP * VIDS), 1, MOST + 1)
    chosen = jax.random.randint(place_key, (), 0, MICRO * N_DP * VIDS)
    flat_counts = counts.reshape(-1)
    flat_counts = jnp.where(jnp.arange(MICRO * N_DP * VIDS) == chosen, MOST, flat_counts)
    return flat_counts.reshape(MICRO, N_DP * VIDS).astype(jnp.int32)


def raised(entries, own_key, source, target, blocks, factor):
    def block_of(axis_at):
        return (jnp.arange(entries.shape[axis_at]) // (entries.shape[axis_at] // blocks)).reshape((-1,) + (1,) * (entries.ndim - 1 - axis_at))

    first = jax.random.permutation(own_key, blocks)[block_of(target)]
    second = (block_of(target) + blocks // 2) % blocks
    return jnp.where((block_of(source) == first) | (block_of(source) == second), factor * entries, entries)


def steps_of(own_key, shape, cuts, low, high):
    def one(position, blocks):
        steps = jax.random.uniform(jax.random.fold_in(jax.random.fold_in(own_key, 6), position), (blocks,), jnp.float32, low / len(cuts), high / len(cuts))
        return jnp.repeat(jnp.exp(steps), shape[position] // blocks).reshape((-1,) + (1,) * (len(shape) - position - 1))

    factor_of = one(*cuts[0])
    for cut in cuts[1:]:
        factor_of = factor_of * one(*cut)
    return factor_of


def centred(stream_key, dims, deviation, reach, shards=(), kind=jnp.bfloat16):
    level = steps_of(stream_key, dims, shards, -0.22, 0.18) if shards else 1.0
    values = jax.random.normal(stream_key, dims, jnp.float32) * deviation * level
    return jnp.minimum(jnp.maximum(values, -reach), reach).astype(kind)


def noise_with(key, dims, deviation, reach, cuts, heavy, kind=jnp.bfloat16):
    entries = deviation * jax.random.normal(key, dims, jnp.float32)
    if cuts:
        entries = entries * steps_of(key, dims, cuts, -0.22, 0.18)
    return jnp.clip(raised(entries, jax.random.fold_in(key, 3), *heavy), -reach, reach).astype(kind)


def setup_inputs(seed: int = 0) -> dict:
    key_of = jax.random.split(jax.random.key(seed), 8)
    features = centred(key_of[0], (MICRO, ROWS, SIDE, SIDE, CHANNELS), 1.0, 6.0, ((1, 8), (4, 4)))
    clip_counts = draw_clip_counts(jax.random.fold_in(key_of[7], 71), 0)
    conv4_weight = centred(key_of[2], (3, 3, CHANNELS, CHANNELS), (9 * CHANNELS) ** -0.5, 0.09375)
    conv4_bias = centred(key_of[3], (CHANNELS,), 0.5, 3.0, (), jnp.float32)
    conv5_weight = centred(key_of[4], (3, 3, CHANNELS, CHANNELS), (9 * CHANNELS) ** -0.5, 0.09375)
    conv5_bias = centred(key_of[5], (CHANNELS,), 0.5, 3.0, (), jnp.float32)
    cotangent = noise_with(key_of[6], (MICRO, ROWS, SIDE, SIDE, CHANNELS), 1.0, 6.0, ((1, 8), (4, 4)), (1, 4, 8, 2.0))
    return dict(features=features, clip_counts=clip_counts, conv4_weight=conv4_weight, conv4_bias=conv4_bias, conv5_weight=conv5_weight, conv5_bias=conv5_bias, cotangent=cotangent)


@jax.custom_vjp
def low(v):
    return lax.optimization_barrier(v.astype(jnp.bfloat16)).astype(jnp.float32)

@jax.custom_vjp
def low_back(v):
    return v

def low_keep(v):
    return (low(v), None)

def low_pass(kept, grad):
    return (grad,)

def back_keep(v):
    return (v, None)

def back_low(kept, grad):
    return (low(grad),)
low.defvjp(low_keep, low_pass)
low_back.defvjp(back_keep, back_low)

def convolve(field, kernel):
    return lax.conv_general_dilated(field, kernel, (1, 1), 'SAME', dimension_numbers=('NHWC', 'HWIO', 'NHWC'), precision=lax.Precision.HIGHEST)

def reference(features, clip_counts, conv4_weight, conv4_bias, conv5_weight, conv5_bias, cotangent):
    live_count = lax.optimization_barrier(jnp.sum(clip_counts.reshape(MICRO, N_DP, VIDS), axis=2))
    slot_index = jnp.arange(CAP, dtype=jnp.int32)
    slot_mask = (slot_index[None, None, :] < live_count[:, :, None]).astype(jnp.float32)
    slot_mask = slot_mask.reshape(MICRO * ROWS, 1, 1, 1)
    maps_in = features.astype(jnp.float32).reshape(MICRO * ROWS, SIDE, SIDE, CHANNELS)
    grad_out = cotangent.astype(jnp.float32).reshape(MICRO * ROWS, SIDE, SIDE, CHANNELS)

    def forward(field, weight4, bias4, weight5, bias5):
        pre4 = low_back(convolve(field, weight4) + bias4)
        hidden = low(low_back(slot_mask * jax.nn.silu(pre4)))
        pre5 = low_back(convolve(hidden, weight5) + bias5)
        return slot_mask * jax.nn.silu(pre5)
    result, pullback = jax.vjp(forward, maps_in, conv4_weight.astype(jnp.float32), conv4_bias, conv5_weight.astype(jnp.float32), conv5_bias)
    grad_in, grad_w4, grad_b4, grad_w5, grad_b5 = pullback(grad_out)
    shape_out = (MICRO, ROWS, SIDE, SIDE, CHANNELS)
    return (result.reshape(shape_out).astype(jnp.bfloat16), grad_in.reshape(shape_out).astype(jnp.bfloat16), grad_w4, grad_b4, grad_w5, grad_b5)
```

```python
import functools

import jax
import jax.numpy as jnp
from jax import lax
from jax.experimental import pallas as pl
from jax.experimental.pallas import tpu as pltpu
from jax.sharding import PartitionSpec as P

WIDE = 16
SLOTS = 8
BF16 = jnp.bfloat16
F32 = jnp.float32
VMEM_LIMIT = 16 * 1024 * 1024


def swap(value, axis_name, size, bit):
    return lax.ppermute(value, axis_name, [(i, i ^ bit) for i in range(size)])


def zero_edges(shifted):
    rows = shifted.shape[1]
    edge = jnp.zeros((shifted.shape[0], WIDE, shifted.shape[2]), BF16)
    shifted[:, :WIDE, :] = edge
    shifted[:, rows - WIDE :, :] = edge


def put_shifted(shifted, first_clip, lanes_of, value):
    clips, cells, width = value.shape
    flat = value.astype(F32).reshape(clips * cells, width)
    turned = (
        pltpu.roll(flat, 1, 0),
        flat,
        pltpu.roll(flat, clips * cells - 1, 0),
    )
    for tap, one in enumerate(turned):
        shifted[first_clip : first_clip + clips, WIDE : WIDE + cells, lanes_of(tap)] = (
            one.astype(BF16).reshape(clips, cells, width)
        )


def rows_of(shifted, tap):
    clips, rows, width = shifted.shape
    cells = rows - 2 * WIDE
    return shifted[:, tap * WIDE : tap * WIDE + cells, :].reshape(clips * cells, width)


def valid_of(info, clips, cells, side):
    column = lax.broadcasted_iota(jnp.int32, (clips * cells, 1), 0)
    inside = (column % WIDE) < side
    clip = column // cells
    live = clip < 0
    for n in range(clips):
        live = live | ((clip == n) & (info[2 + n] > 0))
    return (inside & live).astype(F32)


def fill_from_quarters(info, shifted, quarters):
    zero_edges(shifted)
    channels = shifted.shape[2] // 3
    share = quarters[0].shape[-1]
    for k, quarter in enumerate(quarters):
        at = (info[0] ^ k) * share

        def lanes(tap, at=at):
            return pl.ds(pl.multiple_of(tap * channels + at, share), share)

        put_shifted(shifted, 0, lanes, quarter[...])


def fill_whole(shifted, field):
    zero_edges(shifted)
    channels = shifted.shape[2] // 3
    share = 128
    for at in range(0, channels, share):

        def lanes(tap, at=at):
            return pl.ds(tap * channels + at, share)

        put_shifted(shifted, 0, lanes, field[:, :, at : at + share])


def forward_dot(shifted, weight_of):
    total = None
    for tap in range(3):
        block = weight_of(tap)
        term = jnp.dot(
            rows_of(shifted, tap),
            block.reshape(-1, block.shape[2]),
            preferred_element_type=F32,
        )
        total = term if total is None else total + term
    return total


def backward_dot(shifted, weight, rows):
    total = None
    for tap in range(3):
        first = 3 * (2 - tap)
        block = jnp.concatenate([weight[first + j, rows, :] for j in (2, 1, 0)], axis=1)
        term = lax.dot_general(
            rows_of(shifted, tap),
            block,
            (((1,), (1,)), ((), ())),
            preferred_element_type=F32,
        )
        total = term if total is None else total + term
    return total


def half_of(half, width):
    return pl.ds(pl.multiple_of(half * width, width), width)


def split_quarters(info, value):
    share = value.shape[1] // 2
    left, right = value[:, :share], value[:, share:]
    odd = (info[0] % 2) == 1
    return jnp.where(odd, right, left), jnp.where(odd, left, right)


def put_halves(info, half, value, kept, sent):
    size = value.shape[1] // 4
    left, right = value[:, : 2 * size], value[:, 2 * size :]
    place = info[1]
    crossed = ((place // 2) % 2) == 1
    low = jnp.where(crossed, right, left)
    high = jnp.where(crossed, left, right)
    first = lax.broadcasted_iota(jnp.int32, low.shape, 1) < size
    evens = jnp.where(first, low, pltpu.roll(high, size, 1))
    odds = jnp.where(first, pltpu.roll(low, size, 1), high)
    odd = (place % 2) == 1
    at = pl.ds(pl.multiple_of((half ^ (place // 4)) * 2 * size, 2 * size), 2 * size)
    shape = kept.shape[:2] + (2 * size,)
    kept[:, :, at] = jnp.where(odd, odds, evens).astype(BF16).reshape(shape)
    sent[:, :, at] = jnp.where(odd, evens, odds).astype(BF16).reshape(shape)


def fill_from_pair(info, shifted, same, other):
    zero_edges(shifted)
    share = same.shape[-1]
    for k, quarter in enumerate((same, other)):
        at = ((info[0] % 2) ^ k) * share

        def lanes(tap, at=at):
            return pl.ds(pl.multiple_of(2 * tap * share + at, share), share)

        put_shifted(shifted, 0, lanes, quarter[...])


def pick_kernel(info, pair, out, sem):
    copy = pltpu.make_async_copy(pair.at[1 - info[0] % 2], out, sem)
    copy.start()
    copy.wait()


def conv4_part_kernel(info, near, q1, weight, partial, rest, shifted, own, sems):
    depth = own.shape[1]

    def part_of(half):
        return weight.at[:, half_of(half, depth), :]

    first = pltpu.make_async_copy(part_of(info[0] // 2), own, sems.at[0])
    second = pltpu.make_async_copy(part_of(1 - info[0] // 2), rest, sems.at[1])
    first.start()
    second.start()
    fill_from_pair(info, shifted, near.at[info[0] % 2], q1)
    first.wait()

    @pl.loop(0, 2)
    def _(half):
        lanes = half_of(half, depth)
        partial[half] = forward_dot(shifted, lambda tap: own[3 * tap : 3 * tap + 3, :, lanes])

    second.wait()


def conv4_kernel(side, info, partial, far, q3, bias, weight, later, *refs):
    hidden, factor, fetched, shifted, sem = refs
    clips, cells, share = q3.shape
    copy = pltpu.make_async_copy(later, fetched, sem)
    copy.start()
    fill_from_pair(info, shifted, far.at[info[0] % 2], q3)
    valid = valid_of(info, clips, cells, side)

    @pl.loop(0, 2)
    def _(half):
        lanes = half_of(half, 2 * share)
        pre = forward_dot(shifted, lambda tap: weight[3 * tap : 3 * tap + 3, :, lanes])
        pre = pre + partial[half] + bias[half]
        sig = jax.nn.sigmoid(pre)
        factor[half] = valid * sig * (1.0 + pre * (1.0 - sig))
        even, odd = split_quarters(info, (valid * pre * sig).astype(BF16))
        pair = half ^ (info[0] // 2)
        hidden[pair] = even.reshape(q3.shape)
        hidden[2 + pair] = odd.reshape(q3.shape)

    copy.wait()


def conv5_kernel(side, info, hidden, c0, c1, c2, c3, bias, weight, *refs):
    o0, o1, o23, slope, kept, sent, shifted, upstream = refs
    clips, cells, share = c1.shape
    fill_from_quarters(info, shifted, (hidden.at[0], hidden.at[2], hidden.at[1], hidden.at[3]))
    for k, quarter in enumerate((c0.at[info[0] % 2], c1, c2.at[info[0] % 2], c3)):
        at = pl.multiple_of((info[0] ^ k) * share, share)
        upstream[:, pl.ds(at, share)] = quarter[...].reshape(clips * cells, share)
    valid = valid_of(info, clips, cells, side)

    @pl.loop(0, 2)
    def _(half):
        lanes = half_of(half, 2 * share)
        pre = forward_dot(shifted, lambda tap: weight[3 * tap : 3 * tap + 3, :, lanes])
        pre = pre + bias[half]
        sig = jax.nn.sigmoid(pre)
        put_outputs(info, half, (valid * pre * sig).astype(BF16), o0, o1, o23)
        cot = upstream[:, lanes].astype(F32)
        down = cot * valid * sig * (1.0 + pre * (1.0 - sig))
        slope[:, :, lanes] = down.astype(BF16).reshape(clips, cells, 2 * share)
        put_halves(info, half, down, kept, sent)


def put_outputs(info, half, value, o0, o1, o23):
    even, odd = split_quarters(info, value)
    even, odd = even.reshape(o0.shape), odd.reshape(o0.shape)

    @pl.when(half == info[0] // 2)
    def _():
        o0[...] = even
        o1[...] = odd

    @pl.when(half != info[0] // 2)
    def _():
        o23[0] = even
        o23[1] = odd


def back5_kernel(info, field, factor, weight, later, slope, kept, sent, fetched, shifted, sem):
    copy = pltpu.make_async_copy(later, fetched, sem)
    copy.start()
    fill_whole(shifted, field)
    width = field.shape[2] // 2

    @pl.loop(0, 2)
    def _(half):
        lanes = half_of(half, width)
        back = backward_dot(shifted, weight, lanes).astype(BF16).astype(F32)
        down = back * factor[half]
        slope[:, :, lanes] = down.astype(BF16).reshape(slope.shape[:2] + (width,))
        put_halves(info, half, down, kept, sent)

    copy.wait()


def back4_kernel(info, field, weight, o0, o1, o23, shifted):
    fill_whole(shifted, field)

    @pl.loop(0, 2)
    def _(half):
        back = backward_dot(shifted, weight, half_of(half, field.shape[2] // 2))
        put_outputs(info, half, back.astype(BF16), o0, o1, o23)


def join_kernel(side, info, p0, p1, far, p3, out):
    clips, cells, share = p0.shape
    for k, one in enumerate((p0, p1, far.at[0], p3)):
        value = one[...].reshape(clips, cells // WIDE, WIDE, share)
        first = pl.multiple_of((info[0] ^ k) * clips, clips)
        out[pl.ds(first, clips)] = value[:, :, :side, :]


def grad_kernel(chunks, sources, by_core, n_maps, info, *refs):
    n_outs = 2 * len(chunks)
    scratch = refs[-3:]
    outs = refs[-3 - n_outs : -3]
    shifted, slopes, turned = scratch
    slope_refs = refs[n_maps : n_maps + 4]
    clips, cells, channels = slope_refs[0].shape
    share = shifted.shape[2] // 6
    rows = clips * cells
    size = channels // 4
    zero_edges(shifted)
    for x_bit, quarter in enumerate(sources):
        for n, (at, index) in enumerate(quarter):

            def lanes(tap, x_bit=x_bit):
                return pl.ds((2 * tap + x_bit) * share, share)

            if by_core:
                index = index ^ (info[0] % 2)
            put_shifted(shifted, n * clips, lanes, refs[at][index])
    for n, one in enumerate(slope_refs):
        slopes[n * rows : (n + 1) * rows, :] = one[...].reshape(rows, channels)
    spare = slopes.shape[0] - 4 * rows
    slopes[4 * rows :, :] = jnp.zeros((spare, channels), BF16)
    turned[...] = slopes[...].T

    def place_of(chunk, u, x_bit):
        order = chunks[chunk][0]
        bits = {"x": x_bit, "a": u & 1, "b": u >> 1}
        return outs[2 * chunk + bits[order[0]]], 2 * bits[order[1]] + bits[order[2]]

    for i in range(3):
        window = jnp.concatenate(
            [rows_of(shifted, i), jnp.zeros((spare, shifted.shape[2]), BF16)], axis=0
        )
        part = jnp.dot(turned[...], window, preferred_element_type=F32).astype(BF16)
        for j in range(3):
            tap = 3 * i + j
            chunk = max(c for c in range(len(chunks)) if chunks[c][1] <= tap)
            first = (tap - chunks[chunk][1]) * size
            for x_bit in range(2):
                lane = (2 * j + x_bit) * share
                for u in range(4):
                    out, slot = place_of(chunk, u, x_bit)
                    out[slot, first : first + size, :] = part[
                        u * size : (u + 1) * size, lane : lane + share
                    ]
    total = jnp.sum(slopes[...].astype(F32), axis=0, keepdims=True)
    total = jnp.broadcast_to(total, (WIDE, channels))
    first = chunks[0][2] * size
    for u in range(4):
        both = total[:, 2 * size * (u // 2) : 2 * size * (u // 2 + 1)]
        row = (pltpu.roll(both, size, 1) if u % 2 else both).astype(BF16)
        for x_bit in range(2):
            out, slot = place_of(0, u, x_bit)
            out[slot, first : first + WIDE, :] = row


def body(sizes, features, clip_counts, conv4_weight, conv4_bias, conv5_weight, conv5_bias, cotangent):
    n_dp, n_pipe = sizes
    place = lax.axis_index("pipe")
    row = lax.axis_index("dp")
    micro, slots, side, _, share = features.shape
    group = micro * slots // n_pipe
    channels = conv4_weight.shape[3]
    cells = side * WIDE
    fine = n_dp // SLOTS
    size = channels // SLOTS

    def over_core(value):
        return swap(value, "pipe", n_pipe, 1)

    def over_x(value):
        return swap(value, "pipe", n_pipe, 2)

    def over_y(value):
        return swap(value, "dp", n_dp, fine)

    def over_a(value):
        return swap(value, "dp", n_dp, 2 * fine)

    def over_b(value):
        return swap(value, "dp", n_dp, 4 * fine)

    steps = {"x": over_x, "a": over_a, "b": over_b}

    live_count = jnp.sum(clip_counts, axis=1)
    slot = place * group + jnp.arange(group, dtype=jnp.int32)
    live = (slot % slots < live_count[slot // slots]).astype(jnp.int32)
    info = jnp.concatenate([jnp.stack([place, row // fine]).astype(jnp.int32), live])

    def wide(maps):
        flat = maps.reshape((micro * slots,) + maps.shape[2:])
        flat = jnp.pad(flat, ((0, 0), (0, 0), (0, WIDE - side), (0, 0)))
        return flat.reshape(micro * slots, cells, share)

    core = place % 2

    def clips_of(flat, start, count):
        return lax.dynamic_slice_in_dim(flat, start * group, count * group, 0)

    flat = wide(features)
    pair_dims = (2, group, cells, share)
    near = clips_of(flat, place - core, 2).reshape(pair_dims)
    far = over_x(clips_of(flat, (place - core) ^ 2, 2).reshape(pair_dims))
    q1 = over_core(clips_of(flat, place ^ 1, 1))

    flat = wide(cotangent)
    cot_near = clips_of(flat, place - core, 2).reshape(pair_dims)
    cot_far = over_x(clips_of(flat, (place - core) ^ 2, 2).reshape(pair_dims))


    weight_t = jax.ShapeDtypeStruct((9, channels, channels), BF16)
    weight4 = pltpu.with_memory_space_constraint(conv4_weight.reshape(weight_t.shape), pltpu.HBM)
    weight5 = pltpu.with_memory_space_constraint(conv5_weight.reshape(weight_t.shape), pltpu.HBM)
    bias4 = conv4_bias.reshape(2, 1, channels // 2)
    bias5 = conv5_bias.reshape(2, 1, channels // 2)
    half = channels // 2

    def shape_of(*dims, kind=BF16):
        return jax.ShapeDtypeStruct(dims, kind)

    quarter_t = shape_of(group, cells, share)
    pair_t = shape_of(2, group, cells, share)
    four_t = shape_of(4, group, cells, share)
    half_t = shape_of(group, cells, half)
    whole_t = shape_of(group, cells, channels)
    factor_t = shape_of(2, group * cells, half, kind=F32)

    vmem = pl.BlockSpec(memory_space=pltpu.VMEM)
    anywhere = pl.BlockSpec(memory_space=pl.ANY)
    hbm = pl.BlockSpec(memory_space=pltpu.HBM)

    def shifted_of(depth):
        return pltpu.VMEM((group, cells + 2 * WIDE, 3 * depth), BF16)

    work = 2 * group * cells * 9 * channels * channels

    def call(kernel, name, grid, in_specs, out_specs, out_shape, scratch=(), after=(), flops=0, limit=VMEM_LIMIT):
        n_in = len(in_specs)

        def run(info, *refs):
            kernel(info, *refs[:n_in], *refs[n_in + len(after) :])

        called = pl.pallas_call(
            run,
            grid_spec=pltpu.PrefetchScalarGridSpec(
                num_scalar_prefetch=1,
                grid=grid,
                in_specs=in_specs + [anywhere] * len(after),
                out_specs=out_specs,
                scratch_shapes=scratch,
            ),
            out_shape=out_shape,
            compiler_params=pltpu.CompilerParams(vmem_limit_bytes=limit),
            cost_estimate=pl.CostEstimate(
                flops=flops, bytes_accessed=0, transcendentals=0
            ),
            name=name,
        )
        return lambda *args: called(info, *args, *after)

    def picked(pair):
        (part,) = call(
            pick_kernel,
            "pick",
            (),
            [anywhere],
            [anywhere],
            [quarter_t],
            [pltpu.SemaphoreType.DMA],
            limit=1024 * 1024,
        )(pair)
        return part

    def kernel_grad(name, chunks, sources, by_core, maps, slopes, after):
        out_shape = []
        for n, (_, _, taps) in enumerate(chunks):
            rows = taps * size + (0 if n else WIDE)
            out_shape += [shape_of(4, rows, share)] * 2
        depth = -(-4 * group * cells // 256) * 256
        return call(
            functools.partial(grad_kernel, chunks, sources, by_core, len(maps)),
            name,
            (),
            [vmem] * (len(maps) + 4),
            [vmem] * len(out_shape),
            out_shape,
            [
                pltpu.VMEM((4 * group, cells + 2 * WIDE, 6 * share), BF16),
                pltpu.VMEM((depth, half), BF16),
                pltpu.VMEM((half, depth), BF16),
            ],
            after,
            flops=work * 0 // 8,
        )(*maps, *slopes)

    def held(name, values, after):
        return pl.pallas_call(
            lambda *refs: None,
            in_specs=[anywhere] * (len(values) + len(after)),
            out_specs=[anywhere] * len(values),
            out_shape=[shape_of(*value.shape) for value in values],
            input_output_aliases={n: n for n in range(len(values))},
            compiler_params=pltpu.CompilerParams(vmem_limit_bytes=1024 * 1024),
            cost_estimate=pl.CostEstimate(flops=0, bytes_accessed=0, transcendentals=0),
            name=name,
        )(*values, *after)

    def sends(blocks, chunks):
        kept, sent = blocks[0::2], blocks[1::2]
        return kept, [steps[chunk[0][0]](one) for chunk, one in zip(chunks, sent)]

    def halved(total, chunk, level, after=()):
        cut = total.shape[0] // 2
        kept, moved = total[:cut], steps[chunk[0][level]](total[cut:])
        if after:
            (kept,) = held("after_step", [kept], after)
        return kept + moved

    def finished(totals, chunks):
        totals = [total[0] for total in totals]
        at = chunks[0][2] * size
        bias = totals[0][at:]
        parts = [totals[0][:at]] + totals[1:]
        parts = [part.reshape(-1, size, share) for part in parts]
        bit = fine // 2
        while bit:
            mine = (row // bit) % 2
            bias = bias + swap(bias, "dp", n_dp, bit)
            for n, part in enumerate(parts):
                cut = part.shape[1] // 2
                sent = lax.dynamic_slice_in_dim(part, (1 - mine) * cut, cut, 1)
                kept = lax.dynamic_slice_in_dim(part, mine * cut, cut, 1)
                parts[n] = kept + swap(sent, "dp", n_dp, bit)
            bit //= 2
        per_dp = channels // n_dp
        own = lax.dynamic_slice_in_dim(bias[0], (row % fine) * per_dp, per_dp, 0)
        grads = jnp.concatenate([part.transpose(0, 2, 1).astype(F32) for part in parts])
        return grads.reshape(3, 3, share, per_dp), own.astype(F32)

    def joined(name, o0, o1, far, o3, after):
        (maps,) = call(
            functools.partial(join_kernel, side),
            name,
            (),
            [vmem] * 4,
            [vmem],
            [shape_of(micro * slots, side, side, share)],
            after=[after],
            flops=work * 0 // 8,
        )(o0, o1, far, o3)
        return maps.reshape(features.shape)

    partial4, rest4 = call(
        conv4_part_kernel,
        "conv4_part",
        (),
        [vmem] * 2 + [hbm],
        [vmem] * 2,
        [factor_t, shape_of(9, half, channels)],
        [
            shifted_of(half),
            pltpu.VMEM((9, half, channels), BF16),
            pltpu.SemaphoreType.DMA((2,)),
        ],
        flops=work * 0 // 8,
    )(near, q1, weight4)
    (far,) = held("after_part", [far], [partial4])
    q3 = over_core(picked(far))
    cot1 = over_core(picked(cot_near))
    near_y = over_y(near)
    far_y = over_y(far)

    hidden, factor4, near5 = call(
        functools.partial(conv4_kernel, side),
        "conv4",
        (),
        [vmem] * 5 + [hbm],
        [vmem] * 3,
        [four_t, factor_t, weight_t],
        [shifted_of(half), pltpu.SemaphoreType.DMA],
        [near_y],
        flops=work * 0 // 8,
    )(partial4, far, q3, bias4, rest4, weight5)
    hidden_y = over_y(hidden)
    (cot_far,) = held("after_conv4", [cot_far], [factor4])
    cots = [cot_near, cot1, cot_far, over_core(picked(cot_far))]

    *outs, slope5, kept5, sent5 = call(
        functools.partial(conv5_kernel, side),
        "conv5",
        (),
        [vmem] * 7,
        [vmem] * 6,
        [quarter_t, quarter_t, pair_t, whole_t, half_t, half_t],
        [shifted_of(channels), pltpu.VMEM((group * cells, channels), BF16)],
        [far_y],
        flops=work * 0 // 8,
    )(hidden, *cots, bias5, near5)
    out_far = over_x(outs[2])
    hidden_core = over_core(hidden[2:])


    kept5_core, across5 = over_core(kept5), over_y(sent5)

    slope4, kept4, sent4, near4 = call(
        back5_kernel,
        "back5",
        (),
        [vmem] * 3 + [hbm],
        [vmem] * 4,
        [whole_t, half_t, half_t, weight_t],
        [shifted_of(channels), pltpu.SemaphoreType.DMA],
        [hidden_core],
        flops=work * 0 // 8,
    )(slope5, factor4, near5, weight4)
    kept4_core, across4 = over_core(kept4), over_y(sent4)

    backs = call(
        back4_kernel,
        "back4",
        (),
        [vmem] * 2,
        [vmem] * 3,
        [quarter_t, quarter_t, pair_t],
        [shifted_of(channels)],
        [kept5_core],
        flops=work * 8 // 8,
    )(slope4, near4)
    back_far = over_x(backs[2])

    across5, hidden_y, out_far = held("after_back", [across5, hidden_y, out_far], [backs[0]])
    out3 = over_core(out_far[1])

    hidden_both, across5_core = over_core(hidden_y[2:]), over_core(across5)

    chunks5 = (("xab", 0, 4), ("axb", 4, 5))
    own, other = 0, 1
    chunks4 = (("axb", 0, 5), ("xab", 5, 4))
    blocks5 = kernel_grad(
        "grad5",
        chunks5,
        (((0, 0), (1, 0), (2, 0), (3, 0)), ((0, 1), (1, 1), (2, 1), (3, 1))),
        False,
        (hidden, hidden_core, hidden_y, hidden_both),
        (kept5, kept5_core, across5, across5_core),
        [out3, kept4_core, backs[0]],
    )
    (across4,) = held("after_grad5", [across4], [blocks5[0], back_far])
    across4_core = over_core(across4)
    blocks4 = kernel_grad(
        "grad4",
        chunks4,
        (((0, own), (0, other), (2, own), (2, other)), ((1, own), (1, other), (3, own), (3, other))),
        True,
        (near, far, near_y, far_y),
        (kept4, kept4_core, across4, across4_core),
        [blocks5[0]],
    )

    kept5, moved5 = sends(blocks5, chunks5)
    kept4, moved4 = sends(blocks4, chunks4)
    a4_0, b4_0 = [kept + moved for kept, moved in zip(kept4, moved4)]
    a4_1 = halved(a4_0, chunks4[0], 1)
    b4_1 = halved(b4_0, chunks4[1], 1)
    a4_2 = halved(a4_1, chunks4[0], 2)
    b4_2 = halved(b4_1, chunks4[1], 2)
    a5_0 = held("after_grad4", kept5[:1], [blocks4[0]])[0] + moved5[0]
    b5_0 = held("after_grad4", kept5[1:], [blocks4[0]])[0] + moved5[1]
    a5_1 = halved(a5_0, chunks5[0], 1, [a4_0])
    b5_1 = halved(b5_0, chunks5[1], 1, [b4_0])
    a5_2 = halved(a5_1, chunks5[0], 2, [b4_1])
    b5_2 = halved(b5_1, chunks5[1], 2, [b4_1])
    out1, = held("after_step", [outs[1]], [b5_0])
    out1_core = over_core(out1)


    back1, back_far = held("after_step", [backs[1], back_far], [a4_0])
    conv5_out = joined("join_out", outs[0], out1_core, out_far, out3, b4_1)
    input_grad = joined(
        "join_grad", backs[0], over_core(back1), back_far, over_core(back_far[1]), b4_0
    )
    grad_w5, grad_b5 = finished([a5_2, b5_2], chunks5)
    grad_w4, grad_b4 = finished([a4_2, b4_2], chunks4)
    return (conv5_out, input_grad, grad_w4, grad_b4, grad_w5, grad_b5)


def solution(mesh):
    sizes = (mesh.shape["dp"], mesh.shape["pipe"])
    return jax.shard_map(
        functools.partial(body, sizes),
        mesh=mesh,
        in_specs=(
            P(None, "dp", None, None, "pipe"),
            P(None, "dp"),
            P(),
            P(),
            P(),
            P(),
            P(None, "dp", None, None, "pipe"),
        ),
        out_specs=(
            P(None, "dp", None, None, "pipe"),
            P(None, "dp", None, None, "pipe"),
            P(None, None, "pipe", "dp"),
            P("dp"),
            P(None, None, "pipe", "dp"),
            P("dp"),
        ),
        check_vma=False,
    )
```

```python
import functools

import jax
import jax.numpy as jnp
from jax import lax
from jax.experimental import pallas as pl
from jax.experimental.pallas import tpu as pltpu
from jax.sharding import PartitionSpec as P

WIDE = 16
SLOTS = 8
BF16 = jnp.bfloat16
F32 = jnp.float32
VMEM_LIMIT = 16 * 1024 * 1024


def swap(value, axis_name, size, bit):
    return lax.ppermute(value, axis_name, [(i, i ^ bit) for i in range(size)])


def zero_edges(shifted):
    rows = shifted.shape[1]
    edge = jnp.zeros((shifted.shape[0], WIDE, shifted.shape[2]), BF16)
    shifted[:, :WIDE, :] = edge
    shifted[:, rows - WIDE :, :] = edge


def put_shifted(shifted, first_clip, lanes_of, value):
    clips, cells, width = value.shape
    flat = value.astype(F32).reshape(clips * cells, width)
    turned = (
        pltpu.roll(flat, 1, 0),
        flat,
        pltpu.roll(flat, clips * cells - 1, 0),
    )
    for tap, one in enumerate(turned):
        shifted[first_clip : first_clip + clips, WIDE : WIDE + cells, lanes_of(tap)] = (
            one.astype(BF16).reshape(clips, cells, width)
        )


def rows_of(shifted, tap):
    clips, rows, width = shifted.shape
    cells = rows - 2 * WIDE
    return shifted[:, tap * WIDE : tap * WIDE + cells, :].reshape(clips * cells, width)


def valid_of(info, clips, cells, side):
    column = lax.broadcasted_iota(jnp.int32, (clips * cells, 1), 0)
    inside = (column % WIDE) < side
    clip = column // cells
    live = clip < 0
    for n in range(clips):
        live = live | ((clip == n) & (info[2 + n] > 0))
    return (inside & live).astype(F32)


def fill_from_quarters(info, shifted, quarters):
    zero_edges(shifted)
    channels = shifted.shape[2] // 3
    share = quarters[0].shape[-1]
    for k, quarter in enumerate(quarters):
        at = (info[0] ^ k) * share

        def lanes(tap, at=at):
            return pl.ds(pl.multiple_of(tap * channels + at, share), share)

        put_shifted(shifted, 0, lanes, quarter[...])


def fill_whole(shifted, field):
    zero_edges(shifted)
    channels = shifted.shape[2] // 3
    share = 128
    for at in range(0, channels, share):

        def lanes(tap, at=at):
            return pl.ds(tap * channels + at, share)

        put_shifted(shifted, 0, lanes, field[:, :, at : at + share])


def forward_dot(shifted, weight_of):
    total = None
    for tap in range(3):
        block = weight_of(tap)
        term = jnp.dot(
            rows_of(shifted, tap),
            block.reshape(-1, block.shape[2]),
            preferred_element_type=F32,
        )
        total = term if total is None else total + term
    return total


def backward_dot(shifted, weight, rows):
    total = None
    for tap in range(3):
        first = 3 * (2 - tap)
        block = jnp.concatenate([weight[first + j, rows, :] for j in (2, 1, 0)], axis=1)
        term = lax.dot_general(
            rows_of(shifted, tap),
            block,
            (((1,), (1,)), ((), ())),
            preferred_element_type=F32,
        )
        total = term if total is None else total + term
    return total


def half_of(half, width):
    return pl.ds(pl.multiple_of(half * width, width), width)


def split_quarters(info, value):
    share = value.shape[1] // 2
    left, right = value[:, :share], value[:, share:]
    odd = (info[0] % 2) == 1
    return jnp.where(odd, right, left), jnp.where(odd, left, right)


def put_pairs(info, half, value, kept, sent):
    size = value.shape[1] // 4
    left, right = value[:, : 2 * size], value[:, 2 * size :]
    place = info[1]
    second = ((place // 2) % 2) == 1
    odd = (place % 2) == 1
    own, other = jnp.where(second, right, left), jnp.where(second, left, right)
    at = pl.ds(pl.multiple_of((half ^ (place // 4)) * 2 * size, 2 * size), 2 * size)
    shape = kept.shape[:2] + (2 * size,)
    for one, out in ((own, kept), (other, sent)):
        ordered = jnp.where(odd, pltpu.roll(one, size, 1), one)
        out[:, :, at] = ordered.astype(BF16).reshape(shape)


def put_halves(info, half, value, kept, sent):
    size = value.shape[1] // 4
    left, right = value[:, : 2 * size], value[:, 2 * size :]
    place = info[1]
    crossed = ((place // 2) % 2) == 1
    low = jnp.where(crossed, right, left)
    high = jnp.where(crossed, left, right)
    first = lax.broadcasted_iota(jnp.int32, low.shape, 1) < size
    evens = jnp.where(first, low, pltpu.roll(high, size, 1))
    odds = jnp.where(first, pltpu.roll(low, size, 1), high)
    odd = (place % 2) == 1
    at = pl.ds(pl.multiple_of((half ^ (place // 4)) * 2 * size, 2 * size), 2 * size)
    shape = kept.shape[:2] + (2 * size,)
    kept[:, :, at] = jnp.where(odd, odds, evens).astype(BF16).reshape(shape)
    sent[:, :, at] = jnp.where(odd, evens, odds).astype(BF16).reshape(shape)


def fill_from_pair(info, shifted, same, other):
    zero_edges(shifted)
    share = same.shape[-1]
    for k, quarter in enumerate((same, other)):
        at = ((info[0] % 2) ^ k) * share

        def lanes(tap, at=at):
            return pl.ds(pl.multiple_of(2 * tap * share + at, share), share)

        put_shifted(shifted, 0, lanes, quarter[...])


def pick_kernel(info, pair, out, sem):
    copy = pltpu.make_async_copy(pair.at[1 - info[0] % 2], out, sem)
    copy.start()
    copy.wait()


def conv4_part_kernel(info, near, q1, weight, partial, rest, shifted, own, sems):
    depth = own.shape[1]

    def part_of(half):
        return weight.at[:, half_of(half, depth), :]

    first = pltpu.make_async_copy(part_of(info[0] // 2), own, sems.at[0])
    second = pltpu.make_async_copy(part_of(1 - info[0] // 2), rest, sems.at[1])
    first.start()
    second.start()
    fill_from_pair(info, shifted, near.at[info[0] % 2], q1)
    first.wait()

    @pl.loop(0, 2)
    def _(half):
        lanes = half_of(half, depth)
        partial[half] = forward_dot(shifted, lambda tap: own[3 * tap : 3 * tap + 3, :, lanes])

    second.wait()


def conv4_kernel(side, info, partial, far, q3, bias, weight, later, *refs):
    hidden, factor, fetched, shifted, sem = refs
    clips, cells, share = q3.shape
    copy = pltpu.make_async_copy(later, fetched, sem)
    copy.start()
    fill_from_pair(info, shifted, far.at[info[0] % 2], q3)
    valid = valid_of(info, clips, cells, side)

    @pl.loop(0, 2)
    def _(half):
        lanes = half_of(half, 2 * share)
        pre = forward_dot(shifted, lambda tap: weight[3 * tap : 3 * tap + 3, :, lanes])
        pre = pre + partial[half] + bias[half]
        sig = jax.nn.sigmoid(pre)
        factor[half] = valid * sig * (1.0 + pre * (1.0 - sig))
        even, odd = split_quarters(info, (valid * pre * sig).astype(BF16))
        pair = half ^ (info[0] // 2)
        hidden[pair] = even.reshape(q3.shape)
        hidden[2 + pair] = odd.reshape(q3.shape)

    copy.wait()


def conv5_kernel(side, info, hidden, c0, c1, c2, c3, bias, weight, *refs):
    o0, o1, o23, slope, kept, sent, shifted, upstream = refs
    clips, cells, share = c1.shape
    fill_from_quarters(info, shifted, (hidden.at[0], hidden.at[2], hidden.at[1], hidden.at[3]))
    for k, quarter in enumerate((c0, c1, c2.at[0], c3.at[0])):
        at = pl.multiple_of((info[0] ^ k) * share, share)
        upstream[:, pl.ds(at, share)] = quarter[...].reshape(clips * cells, share)
    valid = valid_of(info, clips, cells, side)

    @pl.loop(0, 2)
    def _(half):
        lanes = half_of(half, 2 * share)
        pre = forward_dot(shifted, lambda tap: weight[3 * tap : 3 * tap + 3, :, lanes])
        pre = pre + bias[half]
        sig = jax.nn.sigmoid(pre)
        put_outputs(info, half, (valid * pre * sig).astype(BF16), o0, o1, o23)
        cot = upstream[:, lanes].astype(F32)
        down = cot * valid * sig * (1.0 + pre * (1.0 - sig))
        slope[:, :, lanes] = down.astype(BF16).reshape(clips, cells, 2 * share)
        put_halves(info, half, down, kept, sent)


def put_outputs(info, half, value, o0, o1, o23):
    even, odd = split_quarters(info, value)
    even, odd = even.reshape(o0.shape), odd.reshape(o0.shape)

    @pl.when(half == info[0] // 2)
    def _():
        o0[...] = even
        o1[...] = odd

    @pl.when(half != info[0] // 2)
    def _():
        o23[0] = even
        o23[1] = odd


def back5_kernel(info, field, factor, weight, later, slope, kept, sent, fetched, shifted, sem):
    copy = pltpu.make_async_copy(later, fetched, sem)
    copy.start()
    fill_whole(shifted, field)
    width = field.shape[2] // 2

    @pl.loop(0, 2)
    def _(half):
        lanes = half_of(half, width)
        back = backward_dot(shifted, weight, lanes).astype(BF16).astype(F32)
        down = back * factor[half]
        slope[:, :, lanes] = down.astype(BF16).reshape(slope.shape[:2] + (width,))
        put_pairs(info, half, down, kept, sent)

    copy.wait()


def back4_kernel(info, field, weight, o0, o1, o23, shifted):
    fill_whole(shifted, field)

    @pl.loop(0, 2)
    def _(half):
        back = backward_dot(shifted, weight, half_of(half, field.shape[2] // 2))
        put_outputs(info, half, back.astype(BF16), o0, o1, o23)


def join_kernel(side, info, p0, p1, far, p3, out):
    clips, cells, share = p0.shape
    for k, one in enumerate((p0, p1, far.at[0], p3)):
        value = one[...].reshape(clips, cells // WIDE, WIDE, share)
        first = pl.multiple_of((info[0] ^ k) * clips, clips)
        out[pl.ds(first, clips)] = value[:, :, :side, :]


def grad_kernel(chunks, sources, by_core, n_maps, info, *refs):
    n_outs = 2 * len(chunks)
    scratch = refs[-3:]
    outs = refs[-3 - n_outs : -3]
    shifted, slopes, turned = scratch
    slope_refs = refs[n_maps : n_maps + 4]
    clips, cells, channels = slope_refs[0].shape
    share = shifted.shape[2] // 6
    rows = clips * cells
    size = channels // 4
    zero_edges(shifted)
    for x_bit, quarter in enumerate(sources):
        for n, (at, index) in enumerate(quarter):

            def lanes(tap, x_bit=x_bit):
                return pl.ds((2 * tap + x_bit) * share, share)

            if by_core:
                index = index ^ (info[0] % 2)
            put_shifted(shifted, n * clips, lanes, refs[at][index])
    for n, one in enumerate(slope_refs):
        slopes[n * rows : (n + 1) * rows, :] = one[...].reshape(rows, channels)
    spare = slopes.shape[0] - 4 * rows
    slopes[4 * rows :, :] = jnp.zeros((spare, channels), BF16)
    turned[...] = slopes[...].T

    def place_of(chunk, u, x_bit):
        order = chunks[chunk][0]
        bits = {"x": x_bit, "y": u & 1, "a": u & 1, "b": u >> 1}
        return outs[2 * chunk + bits[order[0]]], 2 * bits[order[1]] + bits[order[2]]

    for i in range(3):
        window = jnp.concatenate(
            [rows_of(shifted, i), jnp.zeros((spare, shifted.shape[2]), BF16)], axis=0
        )
        part = jnp.dot(turned[...], window, preferred_element_type=F32).astype(BF16)
        for j in range(3):
            tap = 3 * i + j
            chunk = max(c for c in range(len(chunks)) if chunks[c][1] <= tap)
            first = (tap - chunks[chunk][1]) * size
            for x_bit in range(2):
                lane = (2 * j + x_bit) * share
                for u in range(4):
                    out, slot = place_of(chunk, u, x_bit)
                    out[slot, first : first + size, :] = part[
                        u * size : (u + 1) * size, lane : lane + share
                    ]
    total = jnp.sum(slopes[...].astype(F32), axis=0, keepdims=True)
    total = jnp.broadcast_to(total, (WIDE, channels))
    first = chunks[0][2] * size
    for u in range(4):
        both = total[:, 2 * size * (u // 2) : 2 * size * (u // 2 + 1)]
        row = (pltpu.roll(both, size, 1) if u % 2 else both).astype(BF16)
        for x_bit in range(2):
            out, slot = place_of(0, u, x_bit)
            out[slot, first : first + WIDE, :] = row


def body(sizes, features, clip_counts, conv4_weight, conv4_bias, conv5_weight, conv5_bias, cotangent):
    n_dp, n_pipe = sizes
    place = lax.axis_index("pipe")
    row = lax.axis_index("dp")
    micro, slots, side, _, share = features.shape
    group = micro * slots // n_pipe
    channels = conv4_weight.shape[3]
    cells = side * WIDE
    fine = n_dp // SLOTS
    size = channels // SLOTS

    def over_core(value):
        return swap(value, "pipe", n_pipe, 1)

    def over_x(value):
        return swap(value, "pipe", n_pipe, 2)

    def over_y(value):
        return swap(value, "dp", n_dp, fine)

    def over_a(value):
        return swap(value, "dp", n_dp, 2 * fine)

    def over_b(value):
        return swap(value, "dp", n_dp, 4 * fine)

    steps = {"x": over_x, "y": over_y, "a": over_a, "b": over_b}

    live_count = jnp.sum(clip_counts, axis=1)
    slot = place * group + jnp.arange(group, dtype=jnp.int32)
    live = (slot % slots < live_count[slot // slots]).astype(jnp.int32)
    info = jnp.concatenate([jnp.stack([place, row // fine]).astype(jnp.int32), live])

    def wide(maps):
        flat = maps.reshape((micro * slots,) + maps.shape[2:])
        flat = jnp.pad(flat, ((0, 0), (0, 0), (0, WIDE - side), (0, 0)))
        return flat.reshape(micro * slots, cells, share)

    core = place % 2

    def clips_of(flat, start, count):
        return lax.dynamic_slice_in_dim(flat, start * group, count * group, 0)

    flat = wide(features)
    pair_dims = (2, group, cells, share)
    near = clips_of(flat, place - core, 2).reshape(pair_dims)
    far = over_x(clips_of(flat, (place - core) ^ 2, 2).reshape(pair_dims))
    q1 = over_core(clips_of(flat, place ^ 1, 1))

    flat = wide(cotangent)
    cot_own, cot_other = clips_of(flat, place, 1), clips_of(flat, place ^ 1, 1)
    cot_far = over_x(jnp.stack([clips_of(flat, place ^ 2, 1), clips_of(flat, place ^ 3, 1)]))


    weight_t = jax.ShapeDtypeStruct((9, channels, channels), BF16)
    weight4 = pltpu.with_memory_space_constraint(conv4_weight.reshape(weight_t.shape), pltpu.HBM)
    weight5 = pltpu.with_memory_space_constraint(conv5_weight.reshape(weight_t.shape), pltpu.HBM)
    bias4 = conv4_bias.reshape(2, 1, channels // 2)
    bias5 = conv5_bias.reshape(2, 1, channels // 2)
    half = channels // 2

    def shape_of(*dims, kind=BF16):
        return jax.ShapeDtypeStruct(dims, kind)

    quarter_t = shape_of(group, cells, share)
    pair_t = shape_of(2, group, cells, share)
    four_t = shape_of(4, group, cells, share)
    half_t = shape_of(group, cells, half)
    whole_t = shape_of(group, cells, channels)
    factor_t = shape_of(2, group * cells, half, kind=F32)

    vmem = pl.BlockSpec(memory_space=pltpu.VMEM)
    anywhere = pl.BlockSpec(memory_space=pl.ANY)
    hbm = pl.BlockSpec(memory_space=pltpu.HBM)

    def shifted_of(depth):
        return pltpu.VMEM((group, cells + 2 * WIDE, 3 * depth), BF16)

    work = 2 * group * cells * 9 * channels * channels

    def call(kernel, name, grid, in_specs, out_specs, out_shape, scratch=(), after=(), flops=0, limit=VMEM_LIMIT):
        n_in = len(in_specs)

        def run(info, *refs):
            kernel(info, *refs[:n_in], *refs[n_in + len(after) :])

        called = pl.pallas_call(
            run,
            grid_spec=pltpu.PrefetchScalarGridSpec(
                num_scalar_prefetch=1,
                grid=grid,
                in_specs=in_specs + [anywhere] * len(after),
                out_specs=out_specs,
                scratch_shapes=scratch,
            ),
            out_shape=out_shape,
            compiler_params=pltpu.CompilerParams(vmem_limit_bytes=limit),
            cost_estimate=pl.CostEstimate(
                flops=flops, bytes_accessed=0, transcendentals=0
            ),
            name=name,
        )
        return lambda *args: called(info, *args, *after)

    def picked(pair):
        (part,) = call(
            pick_kernel,
            "pick",
            (),
            [anywhere],
            [anywhere],
            [quarter_t],
            [pltpu.SemaphoreType.DMA],
            limit=1024 * 1024,
        )(pair)
        return part

    def kernel_grad(name, chunks, sources, by_core, maps, slopes, after):
        out_shape = []
        for n, (_, _, taps) in enumerate(chunks):
            rows = taps * size + (0 if n else WIDE)
            out_shape += [shape_of(4, rows, share)] * 2
        depth = -(-4 * group * cells // 256) * 256
        return call(
            functools.partial(grad_kernel, chunks, sources, by_core, len(maps)),
            name,
            (),
            [vmem] * (len(maps) + 4),
            [vmem] * len(out_shape),
            out_shape,
            [
                pltpu.VMEM((4 * group, cells + 2 * WIDE, 6 * share), BF16),
                pltpu.VMEM((depth, half), BF16),
                pltpu.VMEM((half, depth), BF16),
            ],
            after,
            flops=work * 0 // 8,
        )(*maps, *slopes)

    def held(name, values, after):
        return pl.pallas_call(
            lambda *refs: None,
            in_specs=[anywhere] * (len(values) + len(after)),
            out_specs=[anywhere] * len(values),
            out_shape=[shape_of(*value.shape) for value in values],
            input_output_aliases={n: n for n in range(len(values))},
            compiler_params=pltpu.CompilerParams(vmem_limit_bytes=1024 * 1024),
            cost_estimate=pl.CostEstimate(flops=0, bytes_accessed=0, transcendentals=0),
            name=name,
        )(*values, *after)

    def sends(blocks, chunks):
        kept, sent = blocks[0::2], blocks[1::2]
        return kept, [steps[chunk[0][0]](one) for chunk, one in zip(chunks, sent)]

    def halved(total, chunk, level, after=()):
        cut = total.shape[0] // 2
        kept, moved = total[:cut], steps[chunk[0][level]](total[cut:])
        if after:
            (kept,) = held("after_step", [kept], after)
        return kept + moved

    def finished(totals, chunks):
        totals = [total[0] for total in totals]
        at = chunks[0][2] * size
        bias = totals[0][at:]
        parts = [totals[0][:at]] + totals[1:]
        parts = [part.reshape(-1, size, share) for part in parts]
        bit = fine // 2
        while bit:
            mine = (row // bit) % 2
            bias = bias + swap(bias, "dp", n_dp, bit)
            for n, part in enumerate(parts):
                cut = part.shape[1] // 2
                sent = lax.dynamic_slice_in_dim(part, (1 - mine) * cut, cut, 1)
                kept = lax.dynamic_slice_in_dim(part, mine * cut, cut, 1)
                parts[n] = kept + swap(sent, "dp", n_dp, bit)
            bit //= 2
        per_dp = channels // n_dp
        own = lax.dynamic_slice_in_dim(bias[0], (row % fine) * per_dp, per_dp, 0)
        grads = jnp.concatenate([part.transpose(0, 2, 1).astype(F32) for part in parts])
        return grads.reshape(3, 3, share, per_dp), own.astype(F32)

    def joined(name, o0, o1, far, o3, after):
        (maps,) = call(
            functools.partial(join_kernel, side),
            name,
            (),
            [vmem] * 4,
            [vmem],
            [shape_of(micro * slots, side, side, share)],
            after=[after],
            flops=work * 0 // 8,
        )(o0, o1, far, o3)
        return maps.reshape(features.shape)

    partial4, rest4 = call(
        conv4_part_kernel,
        "conv4_part",
        (),
        [vmem] * 2 + [hbm],
        [vmem] * 2,
        [factor_t, shape_of(9, half, channels)],
        [
            shifted_of(half),
            pltpu.VMEM((9, half, channels), BF16),
            pltpu.SemaphoreType.DMA((2,)),
        ],
        [cot_own, cot_other],
        flops=work * 0 // 8,
    )(near, q1, weight4)
    (far,) = held("after_part", [far], [partial4])
    q3 = over_core(picked(far))
    near_a = over_a(near)
    far_a = over_a(far)

    hidden, factor4, near5 = call(
        functools.partial(conv4_kernel, side),
        "conv4",
        (),
        [vmem] * 5 + [hbm],
        [vmem] * 3,
        [four_t, factor_t, weight_t],
        [shifted_of(half), pltpu.SemaphoreType.DMA],
        [near_a],
        flops=work * 0 // 8,
    )(partial4, far, q3, bias4, rest4, weight5)
    hidden_y = over_y(hidden)
    (cot_far,) = held("after_conv4", [cot_far], [factor4])
    cots = [cot_own, over_core(cot_other), cot_far, over_core(cot_far[1:])]

    *outs, slope5, kept5, sent5 = call(
        functools.partial(conv5_kernel, side),
        "conv5",
        (),
        [vmem] * 7,
        [vmem] * 6,
        [quarter_t, quarter_t, pair_t, whole_t, half_t, half_t],
        [shifted_of(channels), pltpu.VMEM((group * cells, channels), BF16)],
        [far_a],
        flops=work * 0 // 8,
    )(hidden, *cots, bias5, near5)
    out_far = over_x(outs[2])
    hidden_core = over_core(hidden[2:])


    kept5_core, across5 = over_core(kept5), over_y(sent5)

    slope4, kept4, sent4, near4 = call(
        back5_kernel,
        "back5",
        (),
        [vmem] * 3 + [hbm],
        [vmem] * 4,
        [whole_t, half_t, half_t, weight_t],
        [shifted_of(channels), pltpu.SemaphoreType.DMA],
        [hidden_core],
        flops=work * 0 // 8,
    )(slope5, factor4, near5, weight4)
    kept4_core, across4 = over_core(kept4), over_a(sent4)

    backs = call(
        back4_kernel,
        "back4",
        (),
        [vmem] * 2,
        [vmem] * 3,
        [quarter_t, quarter_t, pair_t],
        [shifted_of(channels)],
        [kept5_core],
        flops=work * 8 // 8,
    )(slope4, near4)
    back_far = over_x(backs[2])

    across5, hidden_y, out_far = held("after_back", [across5, hidden_y, out_far], [backs[0]])
    out3 = over_core(out_far[1])

    hidden_both, across5_core = over_core(hidden_y[2:]), over_core(across5)

    chunks5 = (("xab", 0, 4), ("axb", 4, 5))
    own, other = 0, 1
    chunks4 = (("xyb", 0, 4), ("yxb", 4, 5))
    blocks5 = kernel_grad(
        "grad5",
        chunks5,
        (((0, 0), (1, 0), (2, 0), (3, 0)), ((0, 1), (1, 1), (2, 1), (3, 1))),
        False,
        (hidden, hidden_core, hidden_y, hidden_both),
        (kept5, kept5_core, across5, across5_core),
        [out3, kept4_core, backs[0]],
    )
    (across4,) = held("after_grad5", [across4], [blocks5[0], back_far])
    across4_core = over_core(across4)
    blocks4 = kernel_grad(
        "grad4",
        chunks4,
        (((0, own), (0, other), (2, own), (2, other)), ((1, own), (1, other), (3, own), (3, other))),
        True,
        (near, far, near_a, far_a),
        (kept4, kept4_core, across4, across4_core),
        [blocks5[0]],
    )

    kept5, moved5 = sends(blocks5, chunks5)
    kept4, moved4 = sends(blocks4, chunks4)
    a4_0, b4_0 = [kept + moved for kept, moved in zip(kept4, moved4)]
    a4_1 = halved(a4_0, chunks4[0], 1)
    b4_1 = halved(b4_0, chunks4[1], 1)
    a4_2 = halved(a4_1, chunks4[0], 2)
    b4_2 = halved(b4_1, chunks4[1], 2)
    a5_0 = held("after_grad4", kept5[:1], [blocks4[0]])[0] + moved5[0]
    b5_0 = held("after_grad4", kept5[1:], [blocks4[0]])[0] + moved5[1]
    a5_1 = halved(a5_0, chunks5[0], 1, [a4_0])
    b5_1 = halved(b5_0, chunks5[1], 1, [b4_0])
    a5_2 = halved(a5_1, chunks5[0], 2, [b4_1])
    b5_2 = halved(b5_1, chunks5[1], 2, [b4_1])
    out1, = held("after_step", [outs[1]], [b5_0])
    out1_core = over_core(out1)


    back1, back_far = held("after_step", [backs[1], back_far], [a4_0])
    conv5_out = joined("join_out", outs[0], out1_core, out_far, out3, b4_1)
    input_grad = joined(
        "join_grad", backs[0], over_core(back1), back_far, over_core(back_far[1]), b4_0
    )
    grad_w5, grad_b5 = finished([a5_2, b5_2], chunks5)
    grad_w4, grad_b4 = finished([a4_2, b4_2], chunks4)
    return (conv5_out, input_grad, grad_w4, grad_b4, grad_w5, grad_b5)


def solution(mesh):
    sizes = (mesh.shape["dp"], mesh.shape["pipe"])
    return jax.shard_map(
        functools.partial(body, sizes),
        mesh=mesh,
        in_specs=(
            P(None, "dp", None, None, "pipe"),
            P(None, "dp"),
            P(),
            P(),
            P(),
            P(),
            P(None, "dp", None, None, "pipe"),
        ),
        out_specs=(
            P(None, "dp", None, None, "pipe"),
            P(None, "dp", None, None, "pipe"),
            P(None, None, "pipe", "dp"),
            P("dp"),
            P(None, None, "pipe", "dp"),
            P("dp"),
        ),
        check_vma=False,
    )
```

```python
import functools

import jax
import jax.numpy as jnp
from jax import lax
from jax.experimental import pallas as pl
from jax.experimental.pallas import tpu as pltpu
from jax.sharding import PartitionSpec as P

WIDE = 16
SLOTS = 8
BF16 = jnp.bfloat16
F32 = jnp.float32
VMEM_LIMIT = 16 * 1024 * 1024


def swap(value, axis_name, size, bit):
    return lax.ppermute(value, axis_name, [(i, i ^ bit) for i in range(size)])


def zero_edges(shifted):
    rows = shifted.shape[1]
    edge = jnp.zeros((shifted.shape[0], WIDE, shifted.shape[2]), BF16)
    shifted[:, :WIDE, :] = edge
    shifted[:, rows - WIDE :, :] = edge


def put_shifted(shifted, first_clip, lanes_of, value):
    clips, cells, width = value.shape
    flat = value.astype(F32).reshape(clips * cells, width)
    turned = (
        pltpu.roll(flat, 1, 0),
        flat,
        pltpu.roll(flat, clips * cells - 1, 0),
    )
    for tap, one in enumerate(turned):
        shifted[first_clip : first_clip + clips, WIDE : WIDE + cells, lanes_of(tap)] = (
            one.astype(BF16).reshape(clips, cells, width)
        )


def rows_of(shifted, tap):
    clips, rows, width = shifted.shape
    cells = rows - 2 * WIDE
    return shifted[:, tap * WIDE : tap * WIDE + cells, :].reshape(clips * cells, width)


def valid_of(info, clips, cells, side):
    column = lax.broadcasted_iota(jnp.int32, (clips * cells, 1), 0)
    inside = (column % WIDE) < side
    clip = column // cells
    live = clip < 0
    for n in range(clips):
        live = live | ((clip == n) & (info[2 + n] > 0))
    return (inside & live).astype(F32)


def fill_from_quarters(info, shifted, quarters):
    zero_edges(shifted)
    channels = shifted.shape[2] // 3
    share = quarters[0].shape[-1]
    for k, quarter in enumerate(quarters):
        at = (info[0] ^ k) * share

        def lanes(tap, at=at):
            return pl.ds(pl.multiple_of(tap * channels + at, share), share)

        put_shifted(shifted, 0, lanes, quarter[...])


def fill_whole(shifted, field):
    zero_edges(shifted)
    channels = shifted.shape[2] // 3
    share = 128
    for at in range(0, channels, share):

        def lanes(tap, at=at):
            return pl.ds(tap * channels + at, share)

        put_shifted(shifted, 0, lanes, field[:, :, at : at + share])


def forward_dot(shifted, weight_of):
    total = None
    for tap in range(3):
        block = weight_of(tap)
        term = jnp.dot(
            rows_of(shifted, tap),
            block.reshape(-1, block.shape[2]),
            preferred_element_type=F32,
        )
        total = term if total is None else total + term
    return total


def backward_dot(shifted, weight, rows):
    total = None
    for tap in range(3):
        first = 3 * (2 - tap)
        block = jnp.concatenate([weight[first + j, rows, :] for j in (2, 1, 0)], axis=1)
        term = lax.dot_general(
            rows_of(shifted, tap),
            block,
            (((1,), (1,)), ((), ())),
            preferred_element_type=F32,
        )
        total = term if total is None else total + term
    return total


def half_of(half, width):
    return pl.ds(pl.multiple_of(half * width, width), width)


def split_quarters(info, value):
    share = value.shape[1] // 2
    left, right = value[:, :share], value[:, share:]
    odd = (info[0] % 2) == 1
    return jnp.where(odd, right, left), jnp.where(odd, left, right)


def put_pairs(info, half, value, kept, sent):
    size = value.shape[1] // 4
    left, right = value[:, : 2 * size], value[:, 2 * size :]
    place = info[1]
    second = ((place // 2) % 2) == 1
    odd = (place % 2) == 1
    own, other = jnp.where(second, right, left), jnp.where(second, left, right)
    at = pl.ds(pl.multiple_of((half ^ (place // 4)) * 2 * size, 2 * size), 2 * size)
    shape = kept.shape[:2] + (2 * size,)
    for one, out in ((own, kept), (other, sent)):
        ordered = jnp.where(odd, pltpu.roll(one, size, 1), one)
        out[:, :, at] = ordered.astype(BF16).reshape(shape)


def put_halves(info, half, value, kept, sent):
    size = value.shape[1] // 4
    left, right = value[:, : 2 * size], value[:, 2 * size :]
    place = info[1]
    crossed = ((place // 2) % 2) == 1
    low = jnp.where(crossed, right, left)
    high = jnp.where(crossed, left, right)
    first = lax.broadcasted_iota(jnp.int32, low.shape, 1) < size
    evens = jnp.where(first, low, pltpu.roll(high, size, 1))
    odds = jnp.where(first, pltpu.roll(low, size, 1), high)
    odd = (place % 2) == 1
    at = pl.ds(pl.multiple_of((half ^ (place // 4)) * 2 * size, 2 * size), 2 * size)
    shape = kept.shape[:2] + (2 * size,)
    kept[:, :, at] = jnp.where(odd, odds, evens).astype(BF16).reshape(shape)
    sent[:, :, at] = jnp.where(odd, evens, odds).astype(BF16).reshape(shape)


def fill_from_pair(info, shifted, same, other):
    zero_edges(shifted)
    share = same.shape[-1]
    for k, quarter in enumerate((same, other)):
        at = ((info[0] % 2) ^ k) * share

        def lanes(tap, at=at):
            return pl.ds(pl.multiple_of(2 * tap * share + at, share), share)

        put_shifted(shifted, 0, lanes, quarter[...])


def pick_kernel(info, pair, out, sem):
    copy = pltpu.make_async_copy(pair.at[1 - info[0] % 2], out, sem)
    copy.start()
    copy.wait()


def conv4_part_kernel(info, near, q1, weight, partial, rest, shifted, own, sems):
    depth = own.shape[1]

    def part_of(half):
        return weight.at[:, half_of(half, depth), :]

    first = pltpu.make_async_copy(part_of(info[0] // 2), own, sems.at[0])
    second = pltpu.make_async_copy(part_of(1 - info[0] // 2), rest, sems.at[1])
    first.start()
    second.start()
    fill_from_pair(info, shifted, near.at[info[0] % 2], q1)
    first.wait()

    @pl.loop(0, 2)
    def _(half):
        lanes = half_of(half, depth)
        partial[half] = forward_dot(shifted, lambda tap: own[3 * tap : 3 * tap + 3, :, lanes])

    second.wait()


def conv4_kernel(side, info, partial, far, q3, bias, weight, later, *refs):
    hidden, factor, fetched, shifted, sem = refs
    clips, cells, share = q3.shape
    copy = pltpu.make_async_copy(later, fetched, sem)
    copy.start()
    fill_from_pair(info, shifted, far.at[info[0] % 2], q3)
    valid = valid_of(info, clips, cells, side)

    @pl.loop(0, 2)
    def _(half):
        lanes = half_of(half, 2 * share)
        pre = forward_dot(shifted, lambda tap: weight[3 * tap : 3 * tap + 3, :, lanes])
        pre = pre + partial[half] + bias[half]
        sig = jax.nn.sigmoid(pre)
        factor[half] = valid * sig * (1.0 + pre * (1.0 - sig))
        even, odd = split_quarters(info, (valid * pre * sig).astype(BF16))
        pair = half ^ (info[0] // 2)
        hidden[pair] = even.reshape(q3.shape)
        hidden[2 + pair] = odd.reshape(q3.shape)

    copy.wait()


def conv5_kernel(side, info, hidden, c0, c1, c2, c3, bias, weight, *refs):
    o0, o1, o23, slope, kept, sent, shifted, upstream = refs
    clips, cells, share = c1.shape
    fill_from_quarters(info, shifted, (hidden.at[0], hidden.at[2], hidden.at[1], hidden.at[3]))
    for k, quarter in enumerate((c0, c1, c2.at[0], c3.at[0])):
        at = pl.multiple_of((info[0] ^ k) * share, share)
        upstream[:, pl.ds(at, share)] = quarter[...].reshape(clips * cells, share)
    valid = valid_of(info, clips, cells, side)

    @pl.loop(0, 2)
    def _(half):
        lanes = half_of(half, 2 * share)
        pre = forward_dot(shifted, lambda tap: weight[3 * tap : 3 * tap + 3, :, lanes])
        pre = pre + bias[half]
        sig = jax.nn.sigmoid(pre)
        put_outputs(info, half, (valid * pre * sig).astype(BF16), o0, o1, o23)
        cot = upstream[:, lanes].astype(F32)
        down = cot * valid * sig * (1.0 + pre * (1.0 - sig))
        slope[:, :, lanes] = down.astype(BF16).reshape(clips, cells, 2 * share)
        put_halves(info, half, down, kept, sent)


def put_outputs(info, half, value, o0, o1, o23):
    even, odd = split_quarters(info, value)
    even, odd = even.reshape(o0.shape), odd.reshape(o0.shape)

    @pl.when(half == info[0] // 2)
    def _():
        o0[...] = even
        o1[...] = odd

    @pl.when(half != info[0] // 2)
    def _():
        o23[0] = even
        o23[1] = odd


def back5_kernel(info, field, factor, weight, later, slope, kept, sent, fetched, shifted, sem):
    copy = pltpu.make_async_copy(later, fetched, sem)
    copy.start()
    fill_whole(shifted, field)
    width = field.shape[2] // 2

    @pl.loop(0, 2)
    def _(half):
        lanes = half_of(half, width)
        back = backward_dot(shifted, weight, lanes).astype(BF16).astype(F32)
        down = back * factor[half]
        slope[:, :, lanes] = down.astype(BF16).reshape(slope.shape[:2] + (width,))
        put_pairs(info, half, down, kept, sent)

    copy.wait()


def back4_kernel(info, field, weight, o0, o1, o23, shifted):
    fill_whole(shifted, field)

    @pl.loop(0, 2)
    def _(half):
        back = backward_dot(shifted, weight, half_of(half, field.shape[2] // 2))
        put_outputs(info, half, back.astype(BF16), o0, o1, o23)


def join_kernel(side, info, p0, p1, far, p3, out):
    clips, cells, share = p0.shape
    for k, one in enumerate((p0, p1, far.at[0], p3)):
        value = one[...].reshape(clips, cells // WIDE, WIDE, share)
        first = pl.multiple_of((info[0] ^ k) * clips, clips)
        out[pl.ds(first, clips)] = value[:, :, :side, :]


def grad_kernel(chunks, sources, by_core, n_maps, info, *refs):
    n_outs = 2 * len(chunks)
    scratch = refs[-3:]
    outs = refs[-3 - n_outs : -3]
    shifted, slopes, turned = scratch
    slope_refs = refs[n_maps : n_maps + 4]
    clips, cells, channels = slope_refs[0].shape
    share = shifted.shape[2] // 6
    rows = clips * cells
    size = channels // 4
    zero_edges(shifted)
    for x_bit, quarter in enumerate(sources):
        for n, (at, index) in enumerate(quarter):

            def lanes(tap, x_bit=x_bit):
                return pl.ds((2 * tap + x_bit) * share, share)

            if by_core:
                index = index ^ (info[0] % 2)
            put_shifted(shifted, n * clips, lanes, refs[at][index])
    for n, one in enumerate(slope_refs):
        slopes[n * rows : (n + 1) * rows, :] = one[...].reshape(rows, channels)
    spare = slopes.shape[0] - 4 * rows
    slopes[4 * rows :, :] = jnp.zeros((spare, channels), BF16)
    turned[...] = slopes[...].T

    def place_of(chunk, u, x_bit):
        order = chunks[chunk][0]
        bits = {"x": x_bit, "y": u & 1, "a": u & 1, "b": u >> 1}
        return outs[2 * chunk + bits[order[0]]], 2 * bits[order[1]] + bits[order[2]]

    for i in range(3):
        window = jnp.concatenate(
            [rows_of(shifted, i), jnp.zeros((spare, shifted.shape[2]), BF16)], axis=0
        )
        part = jnp.dot(turned[...], window, preferred_element_type=F32).astype(BF16)
        for j in range(3):
            tap = 3 * i + j
            chunk = max(c for c in range(len(chunks)) if chunks[c][1] <= tap)
            first = (tap - chunks[chunk][1]) * size
            for x_bit in range(2):
                lane = (2 * j + x_bit) * share
                for u in range(4):
                    out, slot = place_of(chunk, u, x_bit)
                    out[slot, first : first + size, :] = part[
                        u * size : (u + 1) * size, lane : lane + share
                    ]
    total = jnp.sum(slopes[...].astype(F32), axis=0, keepdims=True)
    total = jnp.broadcast_to(total, (WIDE, channels))
    first = chunks[0][2] * size
    for u in range(4):
        both = total[:, 2 * size * (u // 2) : 2 * size * (u // 2 + 1)]
        row = (pltpu.roll(both, size, 1) if u % 2 else both).astype(BF16)
        for x_bit in range(2):
            out, slot = place_of(0, u, x_bit)
            out[slot, first : first + WIDE, :] = row


def body(sizes, features, clip_counts, conv4_weight, conv4_bias, conv5_weight, conv5_bias, cotangent):
    n_dp, n_pipe = sizes
    place = lax.axis_index("pipe")
    row = lax.axis_index("dp")
    micro, slots, side, _, share = features.shape
    group = micro * slots // n_pipe
    channels = conv4_weight.shape[3]
    cells = side * WIDE
    fine = n_dp // SLOTS
    size = channels // SLOTS

    def over_core(value):
        return swap(value, "pipe", n_pipe, 1)

    def over_x(value):
        return swap(value, "pipe", n_pipe, 2)

    def over_y(value):
        return swap(value, "dp", n_dp, fine)

    def over_a(value):
        return swap(value, "dp", n_dp, 2 * fine)

    def over_b(value):
        return swap(value, "dp", n_dp, 4 * fine)

    steps = {"x": over_x, "y": over_y, "a": over_a, "b": over_b}

    live_count = jnp.sum(clip_counts, axis=1)
    slot = place * group + jnp.arange(group, dtype=jnp.int32)
    live = (slot % slots < live_count[slot // slots]).astype(jnp.int32)
    info = jnp.concatenate([jnp.stack([place, row // fine]).astype(jnp.int32), live])

    def wide(maps):
        flat = maps.reshape((micro * slots,) + maps.shape[2:])
        flat = jnp.pad(flat, ((0, 0), (0, 0), (0, WIDE - side), (0, 0)))
        return flat.reshape(micro * slots, cells, share)

    core = place % 2

    def clips_of(flat, start, count):
        return lax.dynamic_slice_in_dim(flat, start * group, count * group, 0)

    flat = wide(features)
    pair_dims = (2, group, cells, share)
    near = clips_of(flat, place - core, 2).reshape(pair_dims)
    far = over_x(clips_of(flat, (place - core) ^ 2, 2).reshape(pair_dims))
    q1 = over_core(clips_of(flat, place ^ 1, 1))

    flat = wide(cotangent)
    cot_own, cot_other = clips_of(flat, place, 1), clips_of(flat, place ^ 1, 1)
    cot_far = over_x(jnp.stack([clips_of(flat, place ^ 2, 1), clips_of(flat, place ^ 3, 1)]))


    weight_t = jax.ShapeDtypeStruct((9, channels, channels), BF16)
    weight4 = pltpu.with_memory_space_constraint(conv4_weight.reshape(weight_t.shape), pltpu.HBM)
    weight5 = pltpu.with_memory_space_constraint(conv5_weight.reshape(weight_t.shape), pltpu.HBM)
    bias4 = conv4_bias.reshape(2, 1, channels // 2)
    bias5 = conv5_bias.reshape(2, 1, channels // 2)
    half = channels // 2

    def shape_of(*dims, kind=BF16):
        return jax.ShapeDtypeStruct(dims, kind)

    quarter_t = shape_of(group, cells, share)
    pair_t = shape_of(2, group, cells, share)
    four_t = shape_of(4, group, cells, share)
    half_t = shape_of(group, cells, half)
    whole_t = shape_of(group, cells, channels)
    factor_t = shape_of(2, group * cells, half, kind=F32)

    vmem = pl.BlockSpec(memory_space=pltpu.VMEM)
    anywhere = pl.BlockSpec(memory_space=pl.ANY)
    hbm = pl.BlockSpec(memory_space=pltpu.HBM)

    def shifted_of(depth):
        return pltpu.VMEM((group, cells + 2 * WIDE, 3 * depth), BF16)

    work = 2 * group * cells * 9 * channels * channels

    def call(kernel, name, grid, in_specs, out_specs, out_shape, scratch=(), after=(), flops=0, limit=VMEM_LIMIT):
        n_in = len(in_specs)

        def run(info, *refs):
            kernel(info, *refs[:n_in], *refs[n_in + len(after) :])

        called = pl.pallas_call(
            run,
            grid_spec=pltpu.PrefetchScalarGridSpec(
                num_scalar_prefetch=1,
                grid=grid,
                in_specs=in_specs + [anywhere] * len(after),
                out_specs=out_specs,
                scratch_shapes=scratch,
            ),
            out_shape=out_shape,
            compiler_params=pltpu.CompilerParams(vmem_limit_bytes=limit),
            cost_estimate=pl.CostEstimate(
                flops=flops, bytes_accessed=0, transcendentals=0
            ),
            name=name,
        )
        return lambda *args: called(info, *args, *after)

    def picked(pair):
        (part,) = call(
            pick_kernel,
            "pick",
            (),
            [anywhere],
            [anywhere],
            [quarter_t],
            [pltpu.SemaphoreType.DMA],
            limit=1024 * 1024,
        )(pair)
        return part

    def kernel_grad(name, chunks, sources, by_core, maps, slopes, after):
        out_shape = []
        for n, (_, _, taps) in enumerate(chunks):
            rows = taps * size + (0 if n else WIDE)
            out_shape += [shape_of(4, rows, share)] * 2
        depth = -(-4 * group * cells // 256) * 256
        return call(
            functools.partial(grad_kernel, chunks, sources, by_core, len(maps)),
            name,
            (),
            [vmem] * (len(maps) + 4),
            [vmem] * len(out_shape),
            out_shape,
            [
                pltpu.VMEM((4 * group, cells + 2 * WIDE, 6 * share), BF16),
                pltpu.VMEM((depth, half), BF16),
                pltpu.VMEM((half, depth), BF16),
            ],
            after,
            flops=work * 0 // 8,
        )(*maps, *slopes)

    def held(name, values, after):
        return pl.pallas_call(
            lambda *refs: None,
            in_specs=[anywhere] * (len(values) + len(after)),
            out_specs=[anywhere] * len(values),
            out_shape=[shape_of(*value.shape) for value in values],
            input_output_aliases={n: n for n in range(len(values))},
            compiler_params=pltpu.CompilerParams(vmem_limit_bytes=1024 * 1024),
            cost_estimate=pl.CostEstimate(flops=0, bytes_accessed=0, transcendentals=0),
            name=name,
        )(*values, *after)

    def sends(blocks, chunks):
        kept, sent = blocks[0::2], blocks[1::2]
        return kept, [steps[chunk[0][0]](one) for chunk, one in zip(chunks, sent)]

    def halved(total, chunk, level, after=()):
        cut = total.shape[0] // 2
        kept, moved = total[:cut], steps[chunk[0][level]](total[cut:])
        if after:
            (kept,) = held("after_step", [kept], after)
        return kept + moved

    def finished(totals, chunks):
        totals = [total[0] for total in totals]
        at = chunks[0][2] * size
        bias = totals[0][at:]
        parts = [totals[0][:at]] + totals[1:]
        parts = [part.reshape(-1, size, share) for part in parts]
        bit = fine // 2
        while bit:
            mine = (row // bit) % 2
            bias = bias + swap(bias, "dp", n_dp, bit)
            for n, part in enumerate(parts):
                cut = part.shape[1] // 2
                sent = lax.dynamic_slice_in_dim(part, (1 - mine) * cut, cut, 1)
                kept = lax.dynamic_slice_in_dim(part, mine * cut, cut, 1)
                parts[n] = kept + swap(sent, "dp", n_dp, bit)
            bit //= 2
        per_dp = channels // n_dp
        own = lax.dynamic_slice_in_dim(bias[0], (row % fine) * per_dp, per_dp, 0)
        grads = jnp.concatenate([part.transpose(0, 2, 1).astype(F32) for part in parts])
        return grads.reshape(3, 3, share, per_dp), own.astype(F32)

    def joined(name, o0, o1, far, o3, after):
        (maps,) = call(
            functools.partial(join_kernel, side),
            name,
            (),
            [vmem] * 4,
            [vmem],
            [shape_of(micro * slots, side, side, share)],
            after=[after],
            flops=work * 0 // 8,
        )(o0, o1, far, o3)
        return maps.reshape(features.shape)

    partial4, rest4 = call(
        conv4_part_kernel,
        "conv4_part",
        (),
        [vmem] * 2 + [hbm],
        [vmem] * 2,
        [factor_t, shape_of(9, half, channels)],
        [
            shifted_of(half),
            pltpu.VMEM((9, half, channels), BF16),
            pltpu.SemaphoreType.DMA((2,)),
        ],
        [cot_own, cot_other],
        flops=work * 0 // 8,
    )(near, q1, weight4)
    (far,) = held("after_part", [far], [partial4])
    q3 = over_core(picked(far))
    near_a = over_a(near)
    far_a = over_a(far)

    hidden, factor4, near5 = call(
        functools.partial(conv4_kernel, side),
        "conv4",
        (),
        [vmem] * 5 + [hbm],
        [vmem] * 3,
        [four_t, factor_t, weight_t],
        [shifted_of(half), pltpu.SemaphoreType.DMA],
        [near_a],
        flops=work * 0 // 8,
    )(partial4, far, q3, bias4, rest4, weight5)
    hidden_y = over_y(hidden)
    (cot_far,) = held("after_conv4", [cot_far], [factor4])
    cots = [cot_own, over_core(cot_other), cot_far, over_core(cot_far[1:])]

    *outs, slope5, kept5, sent5 = call(
        functools.partial(conv5_kernel, side),
        "conv5",
        (),
        [vmem] * 7,
        [vmem] * 6,
        [quarter_t, quarter_t, pair_t, whole_t, half_t, half_t],
        [shifted_of(channels), pltpu.VMEM((group * cells, channels), BF16)],
        [],
        flops=work * 0 // 8,
    )(hidden, *cots, bias5, near5)
    out_far = over_x(outs[2])
    hidden_core = over_core(hidden[2:])


    kept5_core, across5 = over_core(kept5), over_y(sent5)

    slope4, kept4, sent4, near4 = call(
        back5_kernel,
        "back5",
        (),
        [vmem] * 3 + [hbm],
        [vmem] * 4,
        [whole_t, half_t, half_t, weight_t],
        [shifted_of(channels), pltpu.SemaphoreType.DMA],
        [far_a, hidden_core],
        flops=work * 0 // 8,
    )(slope5, factor4, near5, weight4)
    kept4_core, across4 = over_core(kept4), over_a(sent4)

    backs = call(
        back4_kernel,
        "back4",
        (),
        [vmem] * 2,
        [vmem] * 3,
        [quarter_t, quarter_t, pair_t],
        [shifted_of(channels)],
        [kept5_core],
        flops=work * 4 // 8,
    )(slope4, near4)
    back_far = over_x(backs[2])

    across5, hidden_y, out_far = held("after_back", [across5, hidden_y, out_far], [backs[0]])
    out3 = over_core(out_far[1])

    hidden_both, across5_core = over_core(hidden_y[2:]), over_core(across5)

    chunks5 = (("xab", 0, 4), ("axb", 4, 5))
    own, other = 0, 1
    chunks4 = (("xyb", 0, 4), ("yxb", 4, 5))
    blocks5 = kernel_grad(
        "grad5",
        chunks5,
        (((0, 0), (1, 0), (2, 0), (3, 0)), ((0, 1), (1, 1), (2, 1), (3, 1))),
        False,
        (hidden, hidden_core, hidden_y, hidden_both),
        (kept5, kept5_core, across5, across5_core),
        [out3, kept4_core, backs[0]],
    )
    (across4,) = held("after_grad5", [across4], [blocks5[0], back_far])
    across4_core = over_core(across4)
    blocks4 = kernel_grad(
        "grad4",
        chunks4,
        (((0, own), (0, other), (2, own), (2, other)), ((1, own), (1, other), (3, own), (3, other))),
        True,
        (near, far, near_a, far_a),
        (kept4, kept4_core, across4, across4_core),
        [blocks5[0]],
    )

    kept5, moved5 = sends(blocks5, chunks5)
    kept4, moved4 = sends(blocks4, chunks4)
    a4_0, b4_0 = [kept + moved for kept, moved in zip(kept4, moved4)]
    a4_1 = halved(a4_0, chunks4[0], 1)
    b4_1 = halved(b4_0, chunks4[1], 1)
    a4_2 = halved(a4_1, chunks4[0], 2)
    b4_2 = halved(b4_1, chunks4[1], 2)
    a5_0 = held("after_grad4", kept5[:1], [blocks4[0]])[0] + moved5[0]
    b5_0 = held("after_grad4", kept5[1:], [blocks4[0]])[0] + moved5[1]
    a5_1 = halved(a5_0, chunks5[0], 1, [a4_0])
    b5_1 = halved(b5_0, chunks5[1], 1, [b4_0])
    a5_2 = halved(a5_1, chunks5[0], 2, [b4_1])
    b5_2 = halved(b5_1, chunks5[1], 2, [b4_1])
    out1, = held("after_step", [outs[1]], [b5_0])
    out1_core = over_core(out1)


    back1, back_far = held("after_step", [backs[1], back_far], [a4_0])
    conv5_out = joined("join_out", outs[0], out1_core, out_far, out3, b4_1)
    input_grad = joined(
        "join_grad", backs[0], over_core(back1), back_far, over_core(back_far[1]), b4_0
    )
    grad_w5, grad_b5 = finished([a5_2, b5_2], chunks5)
    grad_w4, grad_b4 = finished([a4_2, b4_2], chunks4)
    return (conv5_out, input_grad, grad_w4, grad_b4, grad_w5, grad_b5)


def solution(mesh):
    sizes = (mesh.shape["dp"], mesh.shape["pipe"])
    return jax.shard_map(
        functools.partial(body, sizes),
        mesh=mesh,
        in_specs=(
            P(None, "dp", None, None, "pipe"),
            P(None, "dp"),
            P(),
            P(),
            P(),
            P(),
            P(None, "dp", None, None, "pipe"),
        ),
        out_specs=(
            P(None, "dp", None, None, "pipe"),
            P(None, "dp", None, None, "pipe"),
            P(None, None, "pipe", "dp"),
            P("dp"),
            P(None, None, "pipe", "dp"),
            P("dp"),
        ),
        check_vma=False,
    )
```

```python
import functools

import jax
import jax.numpy as jnp
from jax import lax
from jax.experimental import pallas as pl
from jax.experimental.pallas import tpu as pltpu
from jax.sharding import PartitionSpec as P

WIDE = 16
SLOTS = 8
BF16 = jnp.bfloat16
F32 = jnp.float32
VMEM_LIMIT = 16 * 1024 * 1024


def swap(value, axis_name, size, bit):
    return lax.ppermute(value, axis_name, [(i, i ^ bit) for i in range(size)])


def zero_edges(shifted):
    rows = shifted.shape[1]
    edge = jnp.zeros((shifted.shape[0], WIDE, shifted.shape[2]), BF16)
    shifted[:, :WIDE, :] = edge
    shifted[:, rows - WIDE :, :] = edge


def put_shifted(shifted, first_clip, lanes_of, value):
    clips, cells, width = value.shape
    flat = value.astype(F32).reshape(clips * cells, width)
    turned = (
        pltpu.roll(flat, 1, 0),
        flat,
        pltpu.roll(flat, clips * cells - 1, 0),
    )
    for tap, one in enumerate(turned):
        shifted[first_clip : first_clip + clips, WIDE : WIDE + cells, lanes_of(tap)] = (
            one.astype(BF16).reshape(clips, cells, width)
        )


def rows_of(shifted, tap):
    clips, rows, width = shifted.shape
    cells = rows - 2 * WIDE
    return shifted[:, tap * WIDE : tap * WIDE + cells, :].reshape(clips * cells, width)


def valid_of(info, clips, cells, side):
    column = lax.broadcasted_iota(jnp.int32, (clips * cells, 1), 0)
    inside = (column % WIDE) < side
    clip = column // cells
    live = clip < 0
    for n in range(clips):
        live = live | ((clip == n) & (info[2 + n] > 0))
    return (inside & live).astype(F32)


def fill_from_quarters(info, shifted, quarters):
    zero_edges(shifted)
    channels = shifted.shape[2] // 3
    share = quarters[0].shape[-1]
    for k, quarter in enumerate(quarters):
        at = (info[0] ^ k) * share

        def lanes(tap, at=at):
            return pl.ds(pl.multiple_of(tap * channels + at, share), share)

        put_shifted(shifted, 0, lanes, quarter[...])


def fill_whole(shifted, field):
    zero_edges(shifted)
    channels = shifted.shape[2] // 3
    share = 128
    for at in range(0, channels, share):

        def lanes(tap, at=at):
            return pl.ds(tap * channels + at, share)

        put_shifted(shifted, 0, lanes, field[:, :, at : at + share])


def forward_dot(shifted, weight_of):
    total = None
    for tap in range(3):
        block = weight_of(tap)
        term = jnp.dot(
            rows_of(shifted, tap),
            block.reshape(-1, block.shape[2]),
            preferred_element_type=F32,
        )
        total = term if total is None else total + term
    return total


def backward_dot(shifted, weight, rows):
    total = None
    for tap in range(3):
        first = 3 * (2 - tap)
        block = jnp.concatenate([weight[first + j, rows, :] for j in (2, 1, 0)], axis=1)
        term = lax.dot_general(
            rows_of(shifted, tap),
            block,
            (((1,), (1,)), ((), ())),
            preferred_element_type=F32,
        )
        total = term if total is None else total + term
    return total


def half_of(half, width):
    return pl.ds(pl.multiple_of(half * width, width), width)


def split_quarters(info, value):
    share = value.shape[1] // 2
    left, right = value[:, :share], value[:, share:]
    odd = (info[0] % 2) == 1
    return jnp.where(odd, right, left), jnp.where(odd, left, right)


def put_pairs(info, half, value, kept, sent):
    size = value.shape[1] // 4
    left, right = value[:, : 2 * size], value[:, 2 * size :]
    place = info[1]
    second = ((place // 2) % 2) == 1
    odd = (place % 2) == 1
    own, other = jnp.where(second, right, left), jnp.where(second, left, right)
    at = pl.ds(pl.multiple_of((half ^ (place // 4)) * 2 * size, 2 * size), 2 * size)
    shape = kept.shape[:2] + (2 * size,)
    for one, out in ((own, kept), (other, sent)):
        ordered = jnp.where(odd, pltpu.roll(one, size, 1), one)
        out[:, :, at] = ordered.astype(BF16).reshape(shape)


def put_halves(info, half, value, kept, sent):
    size = value.shape[1] // 4
    left, right = value[:, : 2 * size], value[:, 2 * size :]
    place = info[1]
    crossed = ((place // 2) % 2) == 1
    low = jnp.where(crossed, right, left)
    high = jnp.where(crossed, left, right)
    first = lax.broadcasted_iota(jnp.int32, low.shape, 1) < size
    evens = jnp.where(first, low, pltpu.roll(high, size, 1))
    odds = jnp.where(first, pltpu.roll(low, size, 1), high)
    odd = (place % 2) == 1
    at = pl.ds(pl.multiple_of((half ^ (place // 4)) * 2 * size, 2 * size), 2 * size)
    shape = kept.shape[:2] + (2 * size,)
    kept[:, :, at] = jnp.where(odd, odds, evens).astype(BF16).reshape(shape)
    sent[:, :, at] = jnp.where(odd, evens, odds).astype(BF16).reshape(shape)


def fill_from_pair(info, shifted, same, other):
    zero_edges(shifted)
    share = same.shape[-1]
    for k, quarter in enumerate((same, other)):
        at = ((info[0] % 2) ^ k) * share

        def lanes(tap, at=at):
            return pl.ds(pl.multiple_of(2 * tap * share + at, share), share)

        put_shifted(shifted, 0, lanes, quarter[...])


def pick_kernel(info, pair, out, sem):
    copy = pltpu.make_async_copy(pair.at[1 - info[0] % 2], out, sem)
    copy.start()
    copy.wait()


def conv4_part_kernel(info, near, q1, weight, partial, rest, shifted, own, sems):
    depth = own.shape[1]

    def part_of(half):
        return weight.at[:, half_of(half, depth), :]

    first = pltpu.make_async_copy(part_of(info[0] // 2), own, sems.at[0])
    second = pltpu.make_async_copy(part_of(1 - info[0] // 2), rest, sems.at[1])
    first.start()
    second.start()
    fill_from_pair(info, shifted, near.at[info[0] % 2], q1)
    first.wait()

    @pl.loop(0, 2)
    def _(half):
        lanes = half_of(half, depth)
        partial[half] = forward_dot(shifted, lambda tap: own[3 * tap : 3 * tap + 3, :, lanes])

    second.wait()


def conv4_kernel(side, info, partial, far, q3, bias, weight, later, *refs):
    hidden, factor, fetched, shifted, sem = refs
    clips, cells, share = q3.shape
    copy = pltpu.make_async_copy(later, fetched, sem)
    copy.start()
    fill_from_pair(info, shifted, far.at[info[0] % 2], q3)
    valid = valid_of(info, clips, cells, side)

    @pl.loop(0, 2)
    def _(half):
        lanes = half_of(half, 2 * share)
        pre = forward_dot(shifted, lambda tap: weight[3 * tap : 3 * tap + 3, :, lanes])
        pre = pre + partial[half] + bias[half]
        sig = jax.nn.sigmoid(pre)
        factor[half] = valid * sig * (1.0 + pre * (1.0 - sig))
        even, odd = split_quarters(info, (valid * pre * sig).astype(BF16))
        pair = half ^ (info[0] // 2)
        hidden[pair] = even.reshape(q3.shape)
        hidden[2 + pair] = odd.reshape(q3.shape)

    copy.wait()


def conv5_kernel(side, info, hidden, c0, c1, c2, c3, bias, weight, *refs):
    o0, o1, o23, slope, kept, sent, shifted, upstream = refs
    clips, cells, share = c1.shape
    fill_from_quarters(info, shifted, (hidden.at[0], hidden.at[2], hidden.at[1], hidden.at[3]))
    for k, quarter in enumerate((c0, c1, c2.at[0], c3.at[0])):
        at = pl.multiple_of((info[0] ^ k) * share, share)
        upstream[:, pl.ds(at, share)] = quarter[...].reshape(clips * cells, share)
    valid = valid_of(info, clips, cells, side)

    @pl.loop(0, 2)
    def _(half):
        lanes = half_of(half, 2 * share)
        pre = forward_dot(shifted, lambda tap: weight[3 * tap : 3 * tap + 3, :, lanes])
        pre = pre + bias[half]
        sig = jax.nn.sigmoid(pre)
        put_outputs(info, half, (valid * pre * sig).astype(BF16), o0, o1, o23)
        cot = upstream[:, lanes].astype(F32)
        down = cot * valid * sig * (1.0 + pre * (1.0 - sig))
        slope[:, :, lanes] = down.astype(BF16).reshape(clips, cells, 2 * share)
        put_halves(info, half, down, kept, sent)


def put_outputs(info, half, value, o0, o1, o23):
    even, odd = split_quarters(info, value)
    even, odd = even.reshape(o0.shape), odd.reshape(o0.shape)

    @pl.when(half == info[0] // 2)
    def _():
        o0[...] = even
        o1[...] = odd

    @pl.when(half != info[0] // 2)
    def _():
        o23[0] = even
        o23[1] = odd


def back5_kernel(info, field, factor, weight, later, slope, kept, sent, fetched, shifted, sem):
    copy = pltpu.make_async_copy(later, fetched, sem)
    copy.start()
    fill_whole(shifted, field)
    width = field.shape[2] // 2

    @pl.loop(0, 2)
    def _(half):
        lanes = half_of(half, width)
        back = backward_dot(shifted, weight, lanes).astype(BF16).astype(F32)
        down = back * factor[half]
        slope[:, :, lanes] = down.astype(BF16).reshape(slope.shape[:2] + (width,))
        put_pairs(info, half, down, kept, sent)

    copy.wait()


def back4_kernel(info, field, weight, o0, o1, o23, shifted):
    fill_whole(shifted, field)

    @pl.loop(0, 2)
    def _(half):
        back = backward_dot(shifted, weight, half_of(half, field.shape[2] // 2))
        put_outputs(info, half, back.astype(BF16), o0, o1, o23)


def join_kernel(side, info, p0, p1, far, p3, out):
    clips, cells, share = p0.shape
    for k, one in enumerate((p0, p1, far.at[0], p3)):
        value = one[...].reshape(clips, cells // WIDE, WIDE, share)
        first = pl.multiple_of((info[0] ^ k) * clips, clips)
        out[pl.ds(first, clips)] = value[:, :, :side, :]


def grad_kernel(chunks, sources, by_core, n_maps, info, *refs):
    n_outs = 2 * len(chunks)
    scratch = refs[-3:]
    outs = refs[-3 - n_outs : -3]
    shifted, slopes, turned = scratch
    slope_refs = refs[n_maps : n_maps + 4]
    clips, cells, channels = slope_refs[0].shape
    share = shifted.shape[2] // 6
    rows = clips * cells
    size = channels // 4
    zero_edges(shifted)
    for x_bit, quarter in enumerate(sources):
        for n, (at, index) in enumerate(quarter):

            def lanes(tap, x_bit=x_bit):
                return pl.ds((2 * tap + x_bit) * share, share)

            if by_core:
                index = index ^ (info[0] % 2)
            put_shifted(shifted, n * clips, lanes, refs[at][index])
    for n, one in enumerate(slope_refs):
        slopes[n * rows : (n + 1) * rows, :] = one[...].reshape(rows, channels)
    spare = slopes.shape[0] - 4 * rows
    slopes[4 * rows :, :] = jnp.zeros((spare, channels), BF16)
    turned[...] = slopes[...].T

    def place_of(chunk, u, x_bit):
        order = chunks[chunk][0]
        bits = {"x": x_bit, "y": u & 1, "a": u & 1, "b": u >> 1}
        return outs[2 * chunk + bits[order[0]]], 2 * bits[order[1]] + bits[order[2]]

    for i in range(3):
        window = jnp.concatenate(
            [rows_of(shifted, i), jnp.zeros((spare, shifted.shape[2]), BF16)], axis=0
        )
        part = jnp.dot(turned[...], window, preferred_element_type=F32).astype(BF16)
        for j in range(3):
            tap = 3 * i + j
            chunk = max(c for c in range(len(chunks)) if chunks[c][1] <= tap)
            first = (tap - chunks[chunk][1]) * size
            for x_bit in range(2):
                lane = (2 * j + x_bit) * share
                for u in range(4):
                    out, slot = place_of(chunk, u, x_bit)
                    out[slot, first : first + size, :] = part[
                        u * size : (u + 1) * size, lane : lane + share
                    ]
    total = jnp.sum(slopes[...].astype(F32), axis=0, keepdims=True)
    total = jnp.broadcast_to(total, (WIDE, channels))
    first = chunks[0][2] * size
    for u in range(4):
        both = total[:, 2 * size * (u // 2) : 2 * size * (u // 2 + 1)]
        row = (pltpu.roll(both, size, 1) if u % 2 else both).astype(BF16)
        for x_bit in range(2):
            out, slot = place_of(0, u, x_bit)
            out[slot, first : first + WIDE, :] = row


def body(sizes, features, clip_counts, conv4_weight, conv4_bias, conv5_weight, conv5_bias, cotangent):
    n_dp, n_pipe = sizes
    place = lax.axis_index("pipe")
    row = lax.axis_index("dp")
    micro, slots, side, _, share = features.shape
    group = micro * slots // n_pipe
    channels = conv4_weight.shape[3]
    cells = side * WIDE
    fine = n_dp // SLOTS
    size = channels // SLOTS

    def over_core(value):
        return swap(value, "pipe", n_pipe, 1)

    def over_x(value):
        return swap(value, "pipe", n_pipe, 2)

    def over_y(value):
        return swap(value, "dp", n_dp, fine)

    def over_a(value):
        return swap(value, "dp", n_dp, 2 * fine)

    def over_b(value):
        return swap(value, "dp", n_dp, 4 * fine)

    steps = {"x": over_x, "y": over_y, "a": over_a, "b": over_b}

    live_count = jnp.sum(clip_counts, axis=1)
    slot = place * group + jnp.arange(group, dtype=jnp.int32)
    live = (slot % slots < live_count[slot // slots]).astype(jnp.int32)
    info = jnp.concatenate([jnp.stack([place, row // fine]).astype(jnp.int32), live])

    def wide(maps):
        flat = maps.reshape((micro * slots,) + maps.shape[2:])
        flat = jnp.pad(flat, ((0, 0), (0, 0), (0, WIDE - side), (0, 0)))
        return flat.reshape(micro * slots, cells, share)

    core = place % 2

    def clips_of(flat, start, count):
        return lax.dynamic_slice_in_dim(flat, start * group, count * group, 0)

    flat = wide(features)
    pair_dims = (2, group, cells, share)
    near = clips_of(flat, place - core, 2).reshape(pair_dims)
    far = over_x(clips_of(flat, (place - core) ^ 2, 2).reshape(pair_dims))
    q1 = over_core(clips_of(flat, place ^ 1, 1))

    flat = wide(cotangent)
    cot_own, cot_other = clips_of(flat, place, 1), clips_of(flat, place ^ 1, 1)
    cot_far = over_x(jnp.stack([clips_of(flat, place ^ 2, 1), clips_of(flat, place ^ 3, 1)]))


    weight_t = jax.ShapeDtypeStruct((9, channels, channels), BF16)
    weight4 = pltpu.with_memory_space_constraint(conv4_weight.reshape(weight_t.shape), pltpu.HBM)
    weight5 = pltpu.with_memory_space_constraint(conv5_weight.reshape(weight_t.shape), pltpu.HBM)
    bias4 = conv4_bias.reshape(2, 1, channels // 2)
    bias5 = conv5_bias.reshape(2, 1, channels // 2)
    half = channels // 2

    def shape_of(*dims, kind=BF16):
        return jax.ShapeDtypeStruct(dims, kind)

    quarter_t = shape_of(group, cells, share)
    pair_t = shape_of(2, group, cells, share)
    four_t = shape_of(4, group, cells, share)
    half_t = shape_of(group, cells, half)
    whole_t = shape_of(group, cells, channels)
    factor_t = shape_of(2, group * cells, half, kind=F32)

    vmem = pl.BlockSpec(memory_space=pltpu.VMEM)
    anywhere = pl.BlockSpec(memory_space=pl.ANY)
    hbm = pl.BlockSpec(memory_space=pltpu.HBM)

    def shifted_of(depth):
        return pltpu.VMEM((group, cells + 2 * WIDE, 3 * depth), BF16)

    work = 2 * group * cells * 9 * channels * channels

    def call(kernel, name, grid, in_specs, out_specs, out_shape, scratch=(), after=(), flops=0, limit=VMEM_LIMIT):
        n_in = len(in_specs)

        def run(info, *refs):
            kernel(info, *refs[:n_in], *refs[n_in + len(after) :])

        called = pl.pallas_call(
            run,
            grid_spec=pltpu.PrefetchScalarGridSpec(
                num_scalar_prefetch=1,
                grid=grid,
                in_specs=in_specs + [anywhere] * len(after),
                out_specs=out_specs,
                scratch_shapes=scratch,
            ),
            out_shape=out_shape,
            compiler_params=pltpu.CompilerParams(vmem_limit_bytes=limit),
            cost_estimate=pl.CostEstimate(
                flops=flops, bytes_accessed=0, transcendentals=0
            ),
            name=name,
        )
        return lambda *args: called(info, *args, *after)

    def picked(pair):
        (part,) = call(
            pick_kernel,
            "pick",
            (),
            [anywhere],
            [anywhere],
            [quarter_t],
            [pltpu.SemaphoreType.DMA],
            limit=1024 * 1024,
        )(pair)
        return part

    def kernel_grad(name, chunks, sources, by_core, maps, slopes, after):
        out_shape = []
        for n, (_, _, taps) in enumerate(chunks):
            rows = taps * size + (0 if n else WIDE)
            out_shape += [shape_of(4, rows, share)] * 2
        depth = -(-4 * group * cells // 256) * 256
        return call(
            functools.partial(grad_kernel, chunks, sources, by_core, len(maps)),
            name,
            (),
            [vmem] * (len(maps) + 4),
            [vmem] * len(out_shape),
            out_shape,
            [
                pltpu.VMEM((4 * group, cells + 2 * WIDE, 6 * share), BF16),
                pltpu.VMEM((depth, half), BF16),
                pltpu.VMEM((half, depth), BF16),
            ],
            after,
            flops=work * 0 // 8,
        )(*maps, *slopes)

    def held(name, values, after):
        return pl.pallas_call(
            lambda *refs: None,
            in_specs=[anywhere] * (len(values) + len(after)),
            out_specs=[anywhere] * len(values),
            out_shape=[shape_of(*value.shape) for value in values],
            input_output_aliases={n: n for n in range(len(values))},
            compiler_params=pltpu.CompilerParams(vmem_limit_bytes=1024 * 1024),
            cost_estimate=pl.CostEstimate(flops=0, bytes_accessed=0, transcendentals=0),
            name=name,
        )(*values, *after)

    def sends(blocks, chunks):
        kept, sent = blocks[0::2], blocks[1::2]
        return kept, [steps[chunk[0][0]](one) for chunk, one in zip(chunks, sent)]

    def halved(total, chunk, level, after=()):
        cut = total.shape[0] // 2
        kept, moved = total[:cut], steps[chunk[0][level]](total[cut:])
        if after:
            (kept,) = held("after_step", [kept], after)
        return kept + moved

    def finished(totals, chunks):
        totals = [total[0] for total in totals]
        at = chunks[0][2] * size
        bias = totals[0][at:]
        parts = [totals[0][:at]] + totals[1:]
        parts = [part.reshape(-1, size, share) for part in parts]
        bit = fine // 2
        while bit:
            mine = (row // bit) % 2
            bias = bias + swap(bias, "dp", n_dp, bit)
            for n, part in enumerate(parts):
                cut = part.shape[1] // 2
                sent = lax.dynamic_slice_in_dim(part, (1 - mine) * cut, cut, 1)
                kept = lax.dynamic_slice_in_dim(part, mine * cut, cut, 1)
                parts[n] = kept + swap(sent, "dp", n_dp, bit)
            bit //= 2
        per_dp = channels // n_dp
        own = lax.dynamic_slice_in_dim(bias[0], (row % fine) * per_dp, per_dp, 0)
        grads = jnp.concatenate([part.transpose(0, 2, 1).astype(F32) for part in parts])
        return grads.reshape(3, 3, share, per_dp), own.astype(F32)

    def joined(name, o0, o1, far, o3, after):
        (maps,) = call(
            functools.partial(join_kernel, side),
            name,
            (),
            [vmem] * 4,
            [vmem],
            [shape_of(micro * slots, side, side, share)],
            after=[after],
            flops=work * 0 // 8,
        )(o0, o1, far, o3)
        return maps.reshape(features.shape)

    partial4, rest4 = call(
        conv4_part_kernel,
        "conv4_part",
        (),
        [vmem] * 2 + [hbm],
        [vmem] * 2,
        [factor_t, shape_of(9, half, channels)],
        [
            shifted_of(half),
            pltpu.VMEM((9, half, channels), BF16),
            pltpu.SemaphoreType.DMA((2,)),
        ],
        [cot_own, cot_other],
        flops=work * 0 // 8,
    )(near, q1, weight4)
    (far,) = held("after_part", [far], [partial4])
    q3 = over_core(picked(far))
    near_a = over_a(near)
    far_a = over_a(far)

    hidden, factor4, near5 = call(
        functools.partial(conv4_kernel, side),
        "conv4",
        (),
        [vmem] * 5 + [hbm],
        [vmem] * 3,
        [four_t, factor_t, weight_t],
        [shifted_of(half), pltpu.SemaphoreType.DMA],
        [near_a],
        flops=work * 0 // 8,
    )(partial4, far, q3, bias4, rest4, weight5)
    hidden_y = over_y(hidden)
    (cot_far,) = held("after_conv4", [cot_far], [factor4])
    cots = [cot_own, over_core(cot_other), cot_far, over_core(cot_far[1:])]

    *outs, slope5, kept5, sent5 = call(
        functools.partial(conv5_kernel, side),
        "conv5",
        (),
        [vmem] * 7,
        [vmem] * 6,
        [quarter_t, quarter_t, pair_t, whole_t, half_t, half_t],
        [shifted_of(channels), pltpu.VMEM((group * cells, channels), BF16)],
        [],
        flops=work * 0 // 8,
    )(hidden, *cots, bias5, near5)
    out_far = over_x(outs[2])
    hidden_core = over_core(hidden[2:])

    out1_core = over_core(outs[1])

    kept5_core, across5 = over_core(kept5), over_y(sent5)

    slope4, kept4, sent4, near4 = call(
        back5_kernel,
        "back5",
        (),
        [vmem] * 3 + [hbm],
        [vmem] * 4,
        [whole_t, half_t, half_t, weight_t],
        [shifted_of(channels), pltpu.SemaphoreType.DMA],
        [far_a, hidden_core],
        flops=work * 0 // 8,
    )(slope5, factor4, near5, weight4)
    kept4_core, across4 = over_core(kept4), over_a(sent4)

    backs = call(
        back4_kernel,
        "back4",
        (),
        [vmem] * 2,
        [vmem] * 3,
        [quarter_t, quarter_t, pair_t],
        [shifted_of(channels)],
        [kept5_core],
        flops=work * 4 // 8,
    )(slope4, near4)
    back_far = over_x(backs[2])

    across5, hidden_y, out_far = held("after_back", [across5, hidden_y, out_far], [backs[0]])
    out3 = over_core(out_far[1])

    hidden_both, across5_core = over_core(hidden_y[2:]), over_core(across5)

    chunks5 = (("axb", 0, 5), ("xab", 5, 4))
    own, other = 0, 1
    chunks4 = (("yxb", 0, 5), ("xyb", 5, 4))
    blocks5 = kernel_grad(
        "grad5",
        chunks5,
        (((0, 0), (1, 0), (2, 0), (3, 0)), ((0, 1), (1, 1), (2, 1), (3, 1))),
        False,
        (hidden, hidden_core, hidden_y, hidden_both),
        (kept5, kept5_core, across5, across5_core),
        [out1_core, out3, kept4_core, backs[0]],
    )
    (across4,) = held("after_grad5", [across4], [blocks5[0]])
    across4_core = over_core(across4)
    blocks4 = kernel_grad(
        "grad4",
        chunks4,
        (((0, own), (0, other), (2, own), (2, other)), ((1, own), (1, other), (3, own), (3, other))),
        True,
        (near, far, near_a, far_a),
        (kept4, kept4_core, across4, across4_core),
        [blocks5[0], back_far],
    )

    kept5, moved5 = sends(blocks5, chunks5)
    kept4, moved4 = sends(blocks4, chunks4)
    a4_0, b4_0 = [kept + moved for kept, moved in zip(kept4, moved4)]
    a4_1 = halved(a4_0, chunks4[0], 1)
    b4_1 = halved(b4_0, chunks4[1], 1)
    a4_2 = halved(a4_1, chunks4[0], 2)
    b4_2 = halved(b4_1, chunks4[1], 2)
    a5_0 = held("after_grad4", kept5[:1], [blocks4[0]])[0] + moved5[0]
    b5_0 = held("after_grad4", kept5[1:], [blocks4[0]])[0] + moved5[1]
    a5_1 = halved(a5_0, chunks5[0], 1, [a4_0])
    b5_1 = halved(b5_0, chunks5[1], 1, [b4_0])
    a5_2 = halved(a5_1, chunks5[0], 2, [b4_1])
    b5_2 = halved(b5_1, chunks5[1], 2, [b4_1])


    back1, back_far = held("after_step", [backs[1], back_far], [a4_0])
    conv5_out = joined("join_out", outs[0], out1_core, out_far, out3, b4_1)
    input_grad = joined(
        "join_grad", backs[0], over_core(back1), back_far, over_core(back_far[1]), b4_0
    )
    grad_w5, grad_b5 = finished([a5_2, b5_2], chunks5)
    grad_w4, grad_b4 = finished([a4_2, b4_2], chunks4)
    return (conv5_out, input_grad, grad_w4, grad_b4, grad_w5, grad_b5)


def solution(mesh):
    sizes = (mesh.shape["dp"], mesh.shape["pipe"])
    return jax.shard_map(
        functools.partial(body, sizes),
        mesh=mesh,
        in_specs=(
            P(None, "dp", None, None, "pipe"),
            P(None, "dp"),
            P(),
            P(),
            P(),
            P(),
            P(None, "dp", None, None, "pipe"),
        ),
        out_specs=(
            P(None, "dp", None, None, "pipe"),
            P(None, "dp", None, None, "pipe"),
            P(None, None, "pipe", "dp"),
            P("dp"),
            P(None, None, "pipe", "dp"),
            P("dp"),
        ),
        check_vma=False,
    )
```

```python
import functools

import jax
import jax.numpy as jnp
from jax import lax
from jax.experimental import pallas as pl
from jax.experimental.pallas import tpu as pltpu
from jax.sharding import PartitionSpec as P

WIDE = 16
SLOTS = 8
BF16 = jnp.bfloat16
F32 = jnp.float32
VMEM_LIMIT = 16 * 1024 * 1024


def swap(value, axis_name, size, bit):
    return lax.ppermute(value, axis_name, [(i, i ^ bit) for i in range(size)])


def zero_edges(shifted):
    rows = shifted.shape[1]
    edge = jnp.zeros((shifted.shape[0], WIDE, shifted.shape[2]), BF16)
    shifted[:, :WIDE, :] = edge
    shifted[:, rows - WIDE :, :] = edge


def put_shifted(shifted, first_clip, lanes_of, value):
    clips, cells, width = value.shape
    flat = value.astype(F32).reshape(clips * cells, width)
    turned = (
        pltpu.roll(flat, 1, 0),
        flat,
        pltpu.roll(flat, clips * cells - 1, 0),
    )
    for tap, one in enumerate(turned):
        shifted[first_clip : first_clip + clips, WIDE : WIDE + cells, lanes_of(tap)] = (
            one.astype(BF16).reshape(clips, cells, width)
        )


def rows_of(shifted, tap):
    clips, rows, width = shifted.shape
    cells = rows - 2 * WIDE
    return shifted[:, tap * WIDE : tap * WIDE + cells, :].reshape(clips * cells, width)


def valid_of(info, clips, cells, side):
    column = lax.broadcasted_iota(jnp.int32, (clips * cells, 1), 0)
    inside = (column % WIDE) < side
    clip = column // cells
    live = clip < 0
    for n in range(clips):
        live = live | ((clip == n) & (info[2 + n] > 0))
    return (inside & live).astype(F32)


def fill_from_quarters(info, shifted, quarters):
    zero_edges(shifted)
    channels = shifted.shape[2] // 3
    share = quarters[0].shape[-1]
    for k, quarter in enumerate(quarters):
        at = (info[0] ^ k) * share

        def lanes(tap, at=at):
            return pl.ds(pl.multiple_of(tap * channels + at, share), share)

        put_shifted(shifted, 0, lanes, quarter[...])


def fill_whole(shifted, field):
    zero_edges(shifted)
    channels = shifted.shape[2] // 3
    share = 128
    for at in range(0, channels, share):

        def lanes(tap, at=at):
            return pl.ds(tap * channels + at, share)

        put_shifted(shifted, 0, lanes, field[:, :, at : at + share])


def forward_dot(shifted, weight_of):
    total = None
    for tap in range(3):
        block = weight_of(tap)
        term = jnp.dot(
            rows_of(shifted, tap),
            block.reshape(-1, block.shape[2]),
            preferred_element_type=F32,
        )
        total = term if total is None else total + term
    return total


def backward_dot(shifted, weight, rows):
    total = None
    for tap in range(3):
        first = 3 * (2 - tap)
        block = jnp.concatenate([weight[first + j, rows, :] for j in (2, 1, 0)], axis=1)
        term = lax.dot_general(
            rows_of(shifted, tap),
            block,
            (((1,), (1,)), ((), ())),
            preferred_element_type=F32,
        )
        total = term if total is None else total + term
    return total


def half_of(half, width):
    return pl.ds(pl.multiple_of(half * width, width), width)


def split_quarters(info, value):
    share = value.shape[1] // 2
    left, right = value[:, :share], value[:, share:]
    odd = (info[0] % 2) == 1
    return jnp.where(odd, right, left), jnp.where(odd, left, right)


def put_pairs(info, half, value, kept, sent):
    size = value.shape[1] // 4
    left, right = value[:, : 2 * size], value[:, 2 * size :]
    place = info[1]
    second = ((place // 2) % 2) == 1
    odd = (place % 2) == 1
    own, other = jnp.where(second, right, left), jnp.where(second, left, right)
    at = pl.ds(pl.multiple_of((half ^ (place // 4)) * 2 * size, 2 * size), 2 * size)
    shape = kept.shape[:2] + (2 * size,)
    for one, out in ((own, kept), (other, sent)):
        ordered = jnp.where(odd, pltpu.roll(one, size, 1), one)
        out[:, :, at] = ordered.astype(BF16).reshape(shape)


def put_halves(info, half, value, kept, sent):
    size = value.shape[1] // 4
    left, right = value[:, : 2 * size], value[:, 2 * size :]
    place = info[1]
    crossed = ((place // 2) % 2) == 1
    low = jnp.where(crossed, right, left)
    high = jnp.where(crossed, left, right)
    first = lax.broadcasted_iota(jnp.int32, low.shape, 1) < size
    evens = jnp.where(first, low, pltpu.roll(high, size, 1))
    odds = jnp.where(first, pltpu.roll(low, size, 1), high)
    odd = (place % 2) == 1
    at = pl.ds(pl.multiple_of((half ^ (place // 4)) * 2 * size, 2 * size), 2 * size)
    shape = kept.shape[:2] + (2 * size,)
    kept[:, :, at] = jnp.where(odd, odds, evens).astype(BF16).reshape(shape)
    sent[:, :, at] = jnp.where(odd, evens, odds).astype(BF16).reshape(shape)


def fill_from_pair(info, shifted, same, other):
    zero_edges(shifted)
    share = same.shape[-1]
    for k, quarter in enumerate((same, other)):
        at = ((info[0] % 2) ^ k) * share

        def lanes(tap, at=at):
            return pl.ds(pl.multiple_of(2 * tap * share + at, share), share)

        put_shifted(shifted, 0, lanes, quarter[...])


def pick_kernel(info, pair, out, sem):
    copy = pltpu.make_async_copy(pair.at[1 - info[0] % 2], out, sem)
    copy.start()
    copy.wait()


def conv4_part_kernel(info, near, q1, weight, partial, rest, shifted, own, sems):
    depth = own.shape[1]

    def part_of(half):
        return weight.at[:, half_of(half, depth), :]

    first = pltpu.make_async_copy(part_of(info[0] // 2), own, sems.at[0])
    second = pltpu.make_async_copy(part_of(1 - info[0] // 2), rest, sems.at[1])
    first.start()
    second.start()
    fill_from_pair(info, shifted, near.at[info[0] % 2], q1)
    first.wait()

    @pl.loop(0, 2)
    def _(half):
        lanes = half_of(half, depth)
        partial[half] = forward_dot(shifted, lambda tap: own[3 * tap : 3 * tap + 3, :, lanes])

    second.wait()


def conv4_kernel(side, info, partial, far, q3, bias, weight, later, *refs):
    hidden, factor, fetched, shifted, sem = refs
    clips, cells, share = q3.shape
    copy = pltpu.make_async_copy(later, fetched, sem)
    copy.start()
    fill_from_pair(info, shifted, far.at[info[0] % 2], q3)
    valid = valid_of(info, clips, cells, side)

    @pl.loop(0, 2)
    def _(half):
        lanes = half_of(half, 2 * share)
        pre = forward_dot(shifted, lambda tap: weight[3 * tap : 3 * tap + 3, :, lanes])
        pre = pre + partial[half] + bias[half]
        sig = jax.nn.sigmoid(pre)
        factor[half] = valid * sig * (1.0 + pre * (1.0 - sig))
        even, odd = split_quarters(info, (valid * pre * sig).astype(BF16))
        pair = half ^ (info[0] // 2)
        hidden[pair] = even.reshape(q3.shape)
        hidden[2 + pair] = odd.reshape(q3.shape)

    copy.wait()


def conv5_kernel(side, info, hidden, c0, c1, c2, c3, bias, weight, *refs):
    o0, o1, o23, slope, kept, sent, shifted, upstream = refs
    clips, cells, share = c1.shape
    fill_from_quarters(info, shifted, (hidden.at[0], hidden.at[2], hidden.at[1], hidden.at[3]))
    for k, quarter in enumerate((c0, c1, c2.at[0], c3.at[0])):
        at = pl.multiple_of((info[0] ^ k) * share, share)
        upstream[:, pl.ds(at, share)] = quarter[...].reshape(clips * cells, share)
    valid = valid_of(info, clips, cells, side)

    @pl.loop(0, 2)
    def _(half):
        lanes = half_of(half, 2 * share)
        pre = forward_dot(shifted, lambda tap: weight[3 * tap : 3 * tap + 3, :, lanes])
        pre = pre + bias[half]
        sig = jax.nn.sigmoid(pre)
        put_outputs(info, half, (valid * pre * sig).astype(BF16), o0, o1, o23)
        cot = upstream[:, lanes].astype(F32)
        down = cot * valid * sig * (1.0 + pre * (1.0 - sig))
        slope[:, :, lanes] = down.astype(BF16).reshape(clips, cells, 2 * share)
        put_halves(info, half, down, kept, sent)


def put_outputs(info, half, value, o0, o1, o23):
    even, odd = split_quarters(info, value)
    even, odd = even.reshape(o0.shape), odd.reshape(o0.shape)

    @pl.when(half == info[0] // 2)
    def _():
        o0[...] = even
        o1[...] = odd

    @pl.when(half != info[0] // 2)
    def _():
        o23[0] = even
        o23[1] = odd


def back5_kernel(info, field, factor, weight, later, slope, kept, sent, fetched, shifted, sem):
    copy = pltpu.make_async_copy(later, fetched, sem)
    copy.start()
    fill_whole(shifted, field)
    width = field.shape[2] // 2

    @pl.loop(0, 2)
    def _(half):
        lanes = half_of(half, width)
        back = backward_dot(shifted, weight, lanes).astype(BF16).astype(F32)
        down = back * factor[half]
        slope[:, :, lanes] = down.astype(BF16).reshape(slope.shape[:2] + (width,))
        put_pairs(info, half, down, kept, sent)

    copy.wait()


def back4_kernel(info, field, weight, o0, o1, o23, shifted):
    fill_whole(shifted, field)

    @pl.loop(0, 2)
    def _(half):
        back = backward_dot(shifted, weight, half_of(half, field.shape[2] // 2))
        put_outputs(info, half, back.astype(BF16), o0, o1, o23)


def join_kernel(side, info, p0, p1, far, p3, out):
    clips, cells, share = p0.shape
    for k, one in enumerate((p0, p1, far.at[0], p3)):
        value = one[...].reshape(clips, cells // WIDE, WIDE, share)
        first = pl.multiple_of((info[0] ^ k) * clips, clips)
        out[pl.ds(first, clips)] = value[:, :, :side, :]


def grad_kernel(chunks, sources, by_core, n_maps, info, *refs):
    n_outs = 2 * len(chunks)
    scratch = refs[-3:]
    outs = refs[-3 - n_outs : -3]
    shifted, slopes, turned = scratch
    slope_refs = refs[n_maps : n_maps + 4]
    clips, cells, channels = slope_refs[0].shape
    share = shifted.shape[2] // 6
    rows = clips * cells
    size = channels // 4
    zero_edges(shifted)
    for x_bit, quarter in enumerate(sources):
        for n, (at, index) in enumerate(quarter):

            def lanes(tap, x_bit=x_bit):
                return pl.ds((2 * tap + x_bit) * share, share)

            if by_core:
                index = index ^ (info[0] % 2)
            put_shifted(shifted, n * clips, lanes, refs[at][index])
    for n, one in enumerate(slope_refs):
        slopes[n * rows : (n + 1) * rows, :] = one[...].reshape(rows, channels)
    spare = slopes.shape[0] - 4 * rows
    slopes[4 * rows :, :] = jnp.zeros((spare, channels), BF16)
    turned[...] = slopes[...].T

    def place_of(chunk, u, x_bit):
        order = chunks[chunk][0]
        bits = {"x": x_bit, "y": u & 1, "a": u & 1, "b": u >> 1}
        return outs[2 * chunk + bits[order[0]]], 2 * bits[order[1]] + bits[order[2]]

    for i in range(3):
        window = jnp.concatenate(
            [rows_of(shifted, i), jnp.zeros((spare, shifted.shape[2]), BF16)], axis=0
        )
        part = jnp.dot(turned[...], window, preferred_element_type=F32).astype(BF16)
        for j in range(3):
            tap = 3 * i + j
            chunk = max(c for c in range(len(chunks)) if chunks[c][1] <= tap)
            first = (tap - chunks[chunk][1]) * size
            for x_bit in range(2):
                lane = (2 * j + x_bit) * share
                for u in range(4):
                    out, slot = place_of(chunk, u, x_bit)
                    out[slot, first : first + size, :] = part[
                        u * size : (u + 1) * size, lane : lane + share
                    ]
    total = jnp.sum(slopes[...].astype(F32), axis=0, keepdims=True)
    total = jnp.broadcast_to(total, (WIDE, channels))
    first = chunks[0][2] * size
    for u in range(4):
        both = total[:, 2 * size * (u // 2) : 2 * size * (u // 2 + 1)]
        row = (pltpu.roll(both, size, 1) if u % 2 else both).astype(BF16)
        for x_bit in range(2):
            out, slot = place_of(0, u, x_bit)
            out[slot, first : first + WIDE, :] = row


def body(sizes, features, clip_counts, conv4_weight, conv4_bias, conv5_weight, conv5_bias, cotangent):
    n_dp, n_pipe = sizes
    place = lax.axis_index("pipe")
    row = lax.axis_index("dp")
    micro, slots, side, _, share = features.shape
    group = micro * slots // n_pipe
    channels = conv4_weight.shape[3]
    cells = side * WIDE
    fine = n_dp // SLOTS
    size = channels // SLOTS

    def over_core(value):
        return swap(value, "pipe", n_pipe, 1)

    def over_x(value):
        return swap(value, "pipe", n_pipe, 2)

    def over_y(value):
        return swap(value, "dp", n_dp, fine)

    def over_a(value):
        return swap(value, "dp", n_dp, 2 * fine)

    def over_b(value):
        return swap(value, "dp", n_dp, 4 * fine)

    steps = {"x": over_x, "y": over_y, "a": over_a, "b": over_b}

    live_count = jnp.sum(clip_counts, axis=1)
    slot = place * group + jnp.arange(group, dtype=jnp.int32)
    live = (slot % slots < live_count[slot // slots]).astype(jnp.int32)
    info = jnp.concatenate([jnp.stack([place, row // fine]).astype(jnp.int32), live])

    def wide(maps):
        flat = maps.reshape((micro * slots,) + maps.shape[2:])
        flat = jnp.pad(flat, ((0, 0), (0, 0), (0, WIDE - side), (0, 0)))
        return flat.reshape(micro * slots, cells, share)

    core = place % 2

    def clips_of(flat, start, count):
        return lax.dynamic_slice_in_dim(flat, start * group, count * group, 0)

    flat = wide(features)
    pair_dims = (2, group, cells, share)
    near = clips_of(flat, place - core, 2).reshape(pair_dims)
    far = over_x(clips_of(flat, (place - core) ^ 2, 2).reshape(pair_dims))
    q1 = over_core(clips_of(flat, place ^ 1, 1))

    flat = wide(cotangent)
    cot_own, cot_other = clips_of(flat, place, 1), clips_of(flat, place ^ 1, 1)
    cot_far = over_x(jnp.stack([clips_of(flat, place ^ 2, 1), clips_of(flat, place ^ 3, 1)]))


    weight_t = jax.ShapeDtypeStruct((9, channels, channels), BF16)
    weight4 = pltpu.with_memory_space_constraint(conv4_weight.reshape(weight_t.shape), pltpu.HBM)
    weight5 = pltpu.with_memory_space_constraint(conv5_weight.reshape(weight_t.shape), pltpu.HBM)
    bias4 = conv4_bias.reshape(2, 1, channels // 2)
    bias5 = conv5_bias.reshape(2, 1, channels // 2)
    half = channels // 2

    def shape_of(*dims, kind=BF16):
        return jax.ShapeDtypeStruct(dims, kind)

    quarter_t = shape_of(group, cells, share)
    pair_t = shape_of(2, group, cells, share)
    four_t = shape_of(4, group, cells, share)
    half_t = shape_of(group, cells, half)
    whole_t = shape_of(group, cells, channels)
    factor_t = shape_of(2, group * cells, half, kind=F32)

    vmem = pl.BlockSpec(memory_space=pltpu.VMEM)
    anywhere = pl.BlockSpec(memory_space=pl.ANY)
    hbm = pl.BlockSpec(memory_space=pltpu.HBM)

    def shifted_of(depth):
        return pltpu.VMEM((group, cells + 2 * WIDE, 3 * depth), BF16)

    work = 2 * group * cells * 9 * channels * channels

    def call(kernel, name, grid, in_specs, out_specs, out_shape, scratch=(), after=(), flops=0, limit=VMEM_LIMIT):
        n_in = len(in_specs)

        def run(info, *refs):
            kernel(info, *refs[:n_in], *refs[n_in + len(after) :])

        called = pl.pallas_call(
            run,
            grid_spec=pltpu.PrefetchScalarGridSpec(
                num_scalar_prefetch=1,
                grid=grid,
                in_specs=in_specs + [anywhere] * len(after),
                out_specs=out_specs,
                scratch_shapes=scratch,
            ),
            out_shape=out_shape,
            compiler_params=pltpu.CompilerParams(vmem_limit_bytes=limit),
            cost_estimate=pl.CostEstimate(
                flops=flops, bytes_accessed=0, transcendentals=0
            ),
            name=name,
        )
        return lambda *args: called(info, *args, *after)

    def picked(pair):
        (part,) = call(
            pick_kernel,
            "pick",
            (),
            [anywhere],
            [anywhere],
            [quarter_t],
            [pltpu.SemaphoreType.DMA],
            limit=1024 * 1024,
        )(pair)
        return part

    def kernel_grad(name, chunks, sources, by_core, maps, slopes, after):
        out_shape = []
        for n, (_, _, taps) in enumerate(chunks):
            rows = taps * size + (0 if n else WIDE)
            out_shape += [shape_of(4, rows, share)] * 2
        depth = -(-4 * group * cells // 256) * 256
        return call(
            functools.partial(grad_kernel, chunks, sources, by_core, len(maps)),
            name,
            (),
            [vmem] * (len(maps) + 4),
            [vmem] * len(out_shape),
            out_shape,
            [
                pltpu.VMEM((4 * group, cells + 2 * WIDE, 6 * share), BF16),
                pltpu.VMEM((depth, half), BF16),
                pltpu.VMEM((half, depth), BF16),
            ],
            after,
            flops=work * 0 // 8,
        )(*maps, *slopes)

    def held(name, values, after):
        return pl.pallas_call(
            lambda *refs: None,
            in_specs=[anywhere] * (len(values) + len(after)),
            out_specs=[anywhere] * len(values),
            out_shape=[shape_of(*value.shape) for value in values],
            input_output_aliases={n: n for n in range(len(values))},
            compiler_params=pltpu.CompilerParams(vmem_limit_bytes=1024 * 1024),
            cost_estimate=pl.CostEstimate(flops=0, bytes_accessed=0, transcendentals=0),
            name=name,
        )(*values, *after)

    def sends(blocks, chunks):
        kept, sent = blocks[0::2], blocks[1::2]
        return kept, [steps[chunk[0][0]](one) for chunk, one in zip(chunks, sent)]

    def halved(total, chunk, level, after=()):
        cut = total.shape[0] // 2
        kept, moved = total[:cut], steps[chunk[0][level]](total[cut:])
        if after:
            (kept,) = held("after_step", [kept], after)
        return kept + moved

    def finished(totals, chunks):
        totals = [total[0] for total in totals]
        at = chunks[0][2] * size
        bias = totals[0][at:]
        parts = [totals[0][:at]] + totals[1:]
        parts = [part.reshape(-1, size, share) for part in parts]
        bit = fine // 2
        while bit:
            mine = (row // bit) % 2
            bias = bias + swap(bias, "dp", n_dp, bit)
            for n, part in enumerate(parts):
                cut = part.shape[1] // 2
                sent = lax.dynamic_slice_in_dim(part, (1 - mine) * cut, cut, 1)
                kept = lax.dynamic_slice_in_dim(part, mine * cut, cut, 1)
                parts[n] = kept + swap(sent, "dp", n_dp, bit)
            bit //= 2
        per_dp = channels // n_dp
        own = bias[0, :per_dp]
        if fine > 1:
            own = lax.dynamic_slice_in_dim(bias[0], (row % fine) * per_dp, per_dp, 0)
        grads = jnp.concatenate([part.transpose(0, 2, 1).astype(F32) for part in parts])
        return grads.reshape(3, 3, share, per_dp), own.astype(F32)

    def joined(name, o0, o1, far, o3, after):
        (maps,) = call(
            functools.partial(join_kernel, side),
            name,
            (),
            [vmem] * 4,
            [vmem],
            [shape_of(micro * slots, side, side, share)],
            after=[after],
            flops=work * 0 // 8,
        )(o0, o1, far, o3)
        return maps.reshape(features.shape)

    partial4, rest4 = call(
        conv4_part_kernel,
        "conv4_part",
        (),
        [vmem] * 2 + [hbm],
        [vmem] * 2,
        [factor_t, shape_of(9, half, channels)],
        [
            shifted_of(half),
            pltpu.VMEM((9, half, channels), BF16),
            pltpu.SemaphoreType.DMA((2,)),
        ],
        [cot_own, cot_other],
        flops=work * 0 // 8,
    )(near, q1, weight4)
    (far,) = held("after_part", [far], [partial4])
    q3 = over_core(picked(far))
    near_a = over_a(near)
    far_a = over_a(far)

    hidden, factor4, near5 = call(
        functools.partial(conv4_kernel, side),
        "conv4",
        (),
        [vmem] * 5 + [hbm],
        [vmem] * 3,
        [four_t, factor_t, weight_t],
        [shifted_of(half), pltpu.SemaphoreType.DMA],
        [near_a],
        flops=work * 0 // 8,
    )(partial4, far, q3, bias4, rest4, weight5)
    hidden_y = over_y(hidden)
    (cot_far,) = held("after_conv4", [cot_far], [factor4])
    cots = [cot_own, over_core(cot_other), cot_far, over_core(cot_far[1:])]

    *outs, slope5, kept5, sent5 = call(
        functools.partial(conv5_kernel, side),
        "conv5",
        (),
        [vmem] * 7,
        [vmem] * 6,
        [quarter_t, quarter_t, pair_t, whole_t, half_t, half_t],
        [shifted_of(channels), pltpu.VMEM((group * cells, channels), BF16)],
        [],
        flops=work * 0 // 8,
    )(hidden, *cots, bias5, near5)
    out_far = over_x(outs[2])
    hidden_core = over_core(hidden[2:])

    out1_core = over_core(outs[1])

    kept5_core, across5 = over_core(kept5), over_y(sent5)

    slope4, kept4, sent4, near4 = call(
        back5_kernel,
        "back5",
        (),
        [vmem] * 3 + [hbm],
        [vmem] * 4,
        [whole_t, half_t, half_t, weight_t],
        [shifted_of(channels), pltpu.SemaphoreType.DMA],
        [far_a, hidden_core],
        flops=work * 0 // 8,
    )(slope5, factor4, near5, weight4)
    kept4_core, across4 = over_core(kept4), over_a(sent4)

    backs = call(
        back4_kernel,
        "back4",
        (),
        [vmem] * 2,
        [vmem] * 3,
        [quarter_t, quarter_t, pair_t],
        [shifted_of(channels)],
        [kept5_core],
        flops=work * 4 // 8,
    )(slope4, near4)
    back_far = over_x(backs[2])

    across5, hidden_y, out_far = held("after_back", [across5, hidden_y, out_far], [backs[0]])
    out3 = over_core(out_far[1])

    hidden_both, across5_core = over_core(hidden_y[2:]), over_core(across5)

    chunks5 = (("axb", 0, 5), ("xab", 5, 4))
    own, other = 0, 1
    chunks4 = (("yxb", 0, 5), ("xyb", 5, 4))
    blocks5 = kernel_grad(
        "grad5",
        chunks5,
        (((0, 0), (1, 0), (2, 0), (3, 0)), ((0, 1), (1, 1), (2, 1), (3, 1))),
        False,
        (hidden, hidden_core, hidden_y, hidden_both),
        (kept5, kept5_core, across5, across5_core),
        [out1_core, out3, kept4_core, backs[0]],
    )
    (across4,) = held("after_grad5", [across4], [blocks5[0]])
    across4_core = over_core(across4)
    blocks4 = kernel_grad(
        "grad4",
        chunks4,
        (((0, own), (0, other), (2, own), (2, other)), ((1, own), (1, other), (3, own), (3, other))),
        True,
        (near, far, near_a, far_a),
        (kept4, kept4_core, across4, across4_core),
        [blocks5[0], back_far],
    )

    kept5, moved5 = sends(blocks5, chunks5)
    kept4, moved4 = sends(blocks4, chunks4)
    a4_0, b4_0 = [kept + moved for kept, moved in zip(kept4, moved4)]
    a4_1 = halved(a4_0, chunks4[0], 1)
    b4_1 = halved(b4_0, chunks4[1], 1)
    a4_2 = halved(a4_1, chunks4[0], 2)
    b4_2 = halved(b4_1, chunks4[1], 2)
    a5_0 = held("after_grad4", kept5[:1], [blocks4[0]])[0] + moved5[0]
    b5_0 = held("after_grad4", kept5[1:], [blocks4[0]])[0] + moved5[1]
    a5_1 = halved(a5_0, chunks5[0], 1, [a4_0])
    b5_1 = halved(b5_0, chunks5[1], 1, [b4_0])
    a5_2 = halved(a5_1, chunks5[0], 2, [b4_1])
    b5_2 = halved(b5_1, chunks5[1], 2, [b4_1])


    back1, back_far = held("after_step", [backs[1], back_far], [a4_0])
    conv5_out = joined("join_out", outs[0], out1_core, out_far, out3, b4_1)
    input_grad = joined(
        "join_grad", backs[0], over_core(back1), back_far, over_core(back_far[1]), b4_0
    )
    grad_w5, grad_b5 = finished([a5_2, b5_2], chunks5)
    grad_w4, grad_b4 = finished([a4_2, b4_2], chunks4)
    return (conv5_out, input_grad, grad_w4, grad_b4, grad_w5, grad_b5)


def solution(mesh):
    sizes = (mesh.shape["dp"], mesh.shape["pipe"])
    return jax.shard_map(
        functools.partial(body, sizes),
        mesh=mesh,
        in_specs=(
            P(None, "dp", None, None, "pipe"),
            P(None, "dp"),
            P(),
            P(),
            P(),
            P(),
            P(None, "dp", None, None, "pipe"),
        ),
        out_specs=(
            P(None, "dp", None, None, "pipe"),
            P(None, "dp", None, None, "pipe"),
            P(None, None, "pipe", "dp"),
            P("dp"),
            P(None, None, "pipe", "dp"),
            P("dp"),
        ),
        check_vma=False,
    )
```
